1024 devices in a mesh: rep: 64 (over z, x_lo), tp: 16 (over x_hi, y, core).
Axes of the slice: x: 4 (x_hi: 2, x_lo: 2; x = x_hi * 2 + x_lo), y: 4, z: 32, core: 2. Of those that a mesh axis runs over, the one named last changes fastest.
Arguments:
- stream_in: bfloat16 [256, 4, 8192], P('rep', None, 'tp'), may hold values from -6 to 6
- queries: bfloat16 [256, 4, 4096], P('rep'), may hold values from -90 to 90
- new_keys: bfloat16 [256, 4, 4, 128], P('rep'), may hold values from -4 to 4
- new_values: bfloat16 [256, 4, 4, 128], P('rep'), may hold values from -4 to 4
- key_cache: bfloat16 [256, 4096, 4, 128], P('rep', 'tp'), may hold values from -4.1 to 4.1
- value_cache: bfloat16 [256, 4096, 4, 128], P('rep', 'tp'), may hold values from -4 to 4
- lengths: int32 [256], P('rep'), may hold values from 2 to 4096
- out_weight: bfloat16 [4096, 8192], P('tp', 'rep'), may hold values from -0.09375 to 0.09375
- norm_gain: bfloat16 [8192], P('tp'), may hold values from 0.5 to 1.5
Outputs:
- stream_out: bfloat16 [256, 4, 8192], P('rep', None, 'tp')
- normed: bfloat16 [256, 4, 8192], P('rep', None, 'tp')
The draws below stay inside these ranges and needn't reach their ends.
All inputs are finite; a program needn't handle non-finite values.
Results may differ from the reference program's by a relative error of at most 0.0065.
Values may be sent and summed in bfloat16 or wider, within the bound.
No kernel may reach another device: no remote copies, remote signals or barrier semaphores. Data moves between devices by JAX's collectives and lax.ppermute only.
A program may use at most 32 MiB of HBM per device.

```python
import math
import jax
import jax.numpy as jnp
from jax import lax

D = 8192
HEADS = 32
KV_HEADS = 4
HD = 128
STEPS = 4
ROWS = 256
CTX = 4096
FEAT = 4096
N_TP = 16


def shared_keys(key):
    base = jax.random.normal(jax.random.fold_in(key, 11), (ROWS, CTX, KV_HEADS, HD), jnp.float32)
    base = jnp.clip(base, -4.0, 4.0)
    return base


def draw_key_cache(key, part):
    return shared_keys(key).astype(jnp.bfloat16)


def draw_queries(key, part):
    drawn = jax.random.normal(jax.random.fold_in(key, 23), (ROWS, STEPS, HEADS * HD), jnp.float32)
    drawn = jnp.clip(drawn, -4.0, 4.0)
    return drawn.astype(jnp.bfloat16)


def plant(values, stream_key, least, top_value):
    longest = values.shape.index(max(values.shape))
    spots = []
    for shift in (0, 1):
        where = [jax.random.randint(jax.random.fold_in(stream_key, axis), (), 0, length) for axis, length in enumerate(values.shape)]
        where[longest] = (where[longest] + shift) % values.shape[longest]
        spots.append(tuple(where))
    return values.at[spots[0]].set(least).at[spots[1]].set(top_value)


def levels(own_key, dims, cuts, low, largest):
    loudness = 1.0
    for position, parts in cuts:
        heights = jax.random.uniform(jax.random.fold_in(jax.random.fold_in(own_key, 6), position), (parts,), jnp.float32, low / len(cuts), largest / len(cuts))
        loudness = loudness * jnp.repeat(jnp.exp(heights), dims[position] // parts).reshape((-1,) + (1,) * (len(dims) - 1 - position))
    return loudness


def centred(own_key, extent, width, bound, shards=(), kind=jnp.bfloat16):
    result = jax.random.normal(own_key, extent, jnp.float32) * width
    if len(shards) > 0:
        result = levels(own_key, extent, shards, -0.22, 0.18) * result
    return jnp.clip(result, min=-bound, max=bound).astype(kind)


def setup_inputs(seed: int = 0) -> dict:
    key_list = jax.random.split(jax.random.key(seed), 10)
    return {
        "stream_in": centred(key_list[0], (ROWS, STEPS, D), 1.0, 6.0, ((0, 64), (2, 16))),
        "queries": draw_queries(jax.random.fold_in(key_list[9], 71), 0),
        "new_keys": centred(key_list[2], (ROWS, STEPS, KV_HEADS, HD), 1.0, 4.0, ((0, 64),)),
        "new_values": centred(key_list[3], (ROWS, STEPS, KV_HEADS, HD), 1.0, 4.0, ((0, 64),)),
        "key_cache": draw_key_cache(jax.random.fold_in(key_list[9], 71), 0),
        "value_cache": centred(key_list[5], (ROWS, CTX, KV_HEADS, HD), 1.0, 4.0, ((0, 64), (1, 16))),
        "lengths": plant(jax.random.randint(key_list[6], (ROWS,), 2, CTX + 1), jax.random.fold_in(key_list[6], 1), 2, CTX).astype(jnp.int32),
        "out_weight": centred(key_list[7], (FEAT, D), FEAT ** -0.5, 0.09375, ((0, 16), (1, 64))),
        "norm_gain": jnp.clip(1.0 + 0.1 * jax.random.normal(key_list[8], (D,), jnp.float32), 0.5, 1.5).astype(jnp.bfloat16),
    }


def attend_row(packed):
    query, key_new, value_new, key_old, value_old, length = packed
    group_size = HEADS // KV_HEADS
    scaling = 1.0 / math.sqrt(HD)
    query_f = query.astype(jnp.float32).reshape(STEPS, KV_HEADS, group_size, HD)
    cached = jnp.einsum('sgjd,pgd->sgjp', query_f, key_old.astype(jnp.float32)) * scaling
    visible = jnp.arange(CTX) < length
    cached = jnp.where(visible[None, None, None, :], cached, -1e+30)
    fresh = jnp.einsum('sgjd,tgd->sgjt', query_f, key_new.astype(jnp.float32)) * scaling
    causal = jnp.arange(STEPS)[None, :] <= jnp.arange(STEPS)[:, None]
    fresh = jnp.where(causal[:, None, None, :], fresh, -1e+30)
    maxima = jnp.maximum(cached.max(-1), fresh.max(-1))
    weights_cached = jnp.exp(cached - maxima[..., None])
    weights_fresh = jnp.exp(fresh - maxima[..., None])
    denominator = weights_cached.sum(-1) + weights_fresh.sum(-1)
    rounded_cached = lax.optimization_barrier(weights_cached.astype(jnp.bfloat16)).astype(jnp.float32)
    rounded_fresh = lax.optimization_barrier(weights_fresh.astype(jnp.bfloat16)).astype(jnp.float32)
    numerator = jnp.einsum('sgjp,pgd->sgjd', rounded_cached, value_old.astype(jnp.float32))
    numerator = numerator + jnp.einsum('sgjt,tgd->sgjd', rounded_fresh, value_new.astype(jnp.float32))
    attended = (numerator / denominator[..., None]).astype(jnp.bfloat16)
    return attended.reshape(STEPS, HEADS * HD)

def reference(stream_in, queries, new_keys, new_values, key_cache, value_cache, lengths, out_weight, norm_gain):
    attended = lax.map(attend_row, (queries, new_keys, new_values, key_cache, value_cache, lengths))
    flat = attended.reshape(ROWS * STEPS, HEADS * HD)
    width_share = HEADS * HD // N_TP
    summed = jnp.zeros((ROWS * STEPS, D), jnp.float32)
    for group_index in range(N_TP):
        lower = group_index * width_share
        partial_value = jnp.dot(flat[:, lower:lower + width_share], out_weight[lower:lower + width_share], preferred_element_type=jnp.float32)
        summed = summed + lax.optimization_barrier(partial_value.astype(jnp.bfloat16)).astype(jnp.float32)
    hidden = stream_in.reshape(ROWS * STEPS, D).astype(jnp.float32) + summed
    inverse = lax.rsqrt(lax.optimization_barrier(jnp.mean(hidden * hidden, axis=1)) + 1e-06)
    normed = hidden * inverse[:, None] * norm_gain.astype(jnp.float32)[None, :]
    stream_out = hidden.astype(jnp.bfloat16).reshape(ROWS, STEPS, D)
    return (stream_out, normed.astype(jnp.bfloat16).reshape(ROWS, STEPS, D))
```

```python
import math

import jax
import jax.numpy as jnp
from jax import lax
from jax.experimental import pallas as pl
from jax.experimental.pallas import tpu as pltpu
from jax.sharding import Mesh
from jax.sharding import PartitionSpec as P

D = 8192
REP = ("ra", "rb", "rc")
FAR = ("ra", "rb")
NEAR = "rc"
MASKED = -1e30
F32, BF16 = jnp.float32, jnp.bfloat16


def exchanged(pieces, axes):
    return lax.all_to_all(pieces, axes, split_axis=0, concat_axis=0, tiled=True)


def permuted(array, axes, count, target):
    return lax.ppermute(array, axes, [(i, target(i)) for i in range(count)])


def dot_rows(a, b):
    return lax.dot_general(a, b, (((1,), (1,)), ((), ())), preferred_element_type=F32)


def stacked(pieces, axis=0):
    return jnp.concatenate(pieces, axis=axis)


def attend_kernel(len_ref, q_ref, nk_ref, nv_ref, k_ref, v_ref, out_ref, stats_ref):
    b = pl.program_id(0)
    rows_b = pl.num_programs(0)
    _, steps, width = q_ref.shape
    head_dim = k_ref.shape[2]
    kv_heads = nk_ref.shape[1] // steps
    heads = width // head_dim
    rows = heads * steps
    columns = k_ref.shape[1]
    block_len = columns // kv_heads
    scaling = 1.0 / math.sqrt(head_dim)
    tp = lax.axis_index("tp")

    def own_head(count):
        row = lax.broadcasted_iota(jnp.int32, (rows, count), 0)
        column = lax.broadcasted_iota(jnp.int32, (rows, count), 1)
        same = (column % kv_heads) == (row // (rows // kv_heads))
        return row, column // kv_heads, same

    _, position, same = own_head(columns)
    visible = same & (position < len_ref[b] - tp * block_len)
    row, fresh_at, same = own_head(nk_ref.shape[1])
    fresh_visible = same & (fresh_at <= row % steps) & (tp == 0)
    wide = q_ref[0].astype(F32)
    q = stacked([wide[:, h * head_dim : (h + 1) * head_dim] for h in range(heads)]).astype(BF16)
    scores = jnp.where(visible, dot_rows(q, k_ref[0]) * scaling, MASKED)
    fresh = jnp.where(fresh_visible, dot_rows(q, nk_ref[0]) * scaling, MASKED)
    top = jnp.maximum(scores.max(1, keepdims=True), fresh.max(1, keepdims=True))
    shift = top.astype(BF16).astype(F32)
    weights = jnp.where(visible, jnp.exp(scores - shift), 0.0)
    fresh_weights = jnp.where(fresh_visible, jnp.exp(fresh - shift), 0.0)
    total = weights.sum(1, keepdims=True) + fresh_weights.sum(1, keepdims=True)
    numerator = jnp.dot(weights.astype(BF16), v_ref[0], preferred_element_type=F32)
    numerator += jnp.dot(fresh_weights.astype(BF16), nv_ref[0], preferred_element_type=F32)
    out_ref[:, b] = numerator.astype(BF16).reshape(-1, 8, head_dim)
    high = total.astype(BF16).astype(F32)
    lane = lax.broadcasted_iota(jnp.int32, (rows, head_dim), 1)
    stats = jnp.where(b == 0, jnp.zeros((rows, head_dim), F32), stats_ref[...])
    stats = jnp.where(lane == 3 * b, shift, stats)
    stats = jnp.where(lane == 3 * b + 1, high, stats)
    stats = jnp.where(lane == 3 * b + 2, total - high, stats)
    stats_ref[...] = stats
    out_ref[:, rows_b] = stats.astype(BF16).reshape(-1, 8, head_dim)


def attend(queries, new_keys, new_values, keys, values, lengths, outs):
    def of_row(a):
        return pl.BlockSpec((1, *a.shape[1:]), lambda b: (b, 0, 0))

    return pl.pallas_call(
        attend_kernel,
        grid=(queries.shape[0],),
        out_shape=outs,
        in_specs=[
            pl.BlockSpec(memory_space=pltpu.SMEM),
            *(of_row(a) for a in (queries, new_keys, new_values, keys, values)),
        ],
        out_specs=pl.BlockSpec(outs.shape, lambda b: (0, 0, 0, 0)),
        scratch_shapes=[pltpu.VMEM((outs.shape[0] * outs.shape[2], outs.shape[3]), F32)],
        compiler_params=pltpu.CompilerParams(vmem_limit_bytes=60 * 1024 * 1024),
        cost_estimate=pl.CostEstimate(
            flops=300_000_000, bytes_accessed=2 * keys.size * 2, transcendentals=600_000
        ),
    )(lengths, queries, new_keys, new_values, keys, values)


def combine_kernel(parts_ref, out_ref):
    rows_b = parts_ref.shape[1] - 1
    half = parts_ref.shape[2] // 2
    stats = parts_ref[:, rows_b].astype(F32)
    first, second = [], []
    for b in range(rows_b):
        shift, high, low = (stats[:, :, 3 * b + i : 3 * b + i + 1] for i in range(3))
        scale = jnp.exp(shift - shift.max(0, keepdims=True))
        total = jnp.sum(scale * (high + low), axis=0)
        numerator = jnp.sum(scale * parts_ref[:, b].astype(F32), axis=0)
        attended = numerator / total
        first.append(attended[:half])
        second.append(attended[half:])
    attended = stacked([stacked(first), stacked(second)], 1).astype(BF16)
    for i in range(out_ref.shape[0]):
        out_ref[i] = attended


def project_kernel(x_ref, w_ref, out_ref):
    x = x_ref[...].reshape(-1, x_ref.shape[2])
    for j in range(w_ref.shape[0]):
        part = jnp.dot(x, w_ref[j], preferred_element_type=F32).astype(BF16)
        out_ref[:, :, j * 128 : (j + 1) * 128] = part.reshape(*out_ref.shape[:2], 128)


def sum_kernel(parts_ref, out_ref):
    out_ref[...] = jnp.sum(parts_ref[...].astype(F32), axis=0).astype(BF16)


def hidden_kernel(summed_ref, stream_ref, hidden_ref, squares_ref):
    stream = stacked([stream_ref[b].astype(F32) for b in range(stream_ref.shape[0])])
    hidden = stream + summed_ref[...].astype(F32)
    hidden_ref[...] = hidden
    squares = hidden * hidden
    squares = sum(squares[:, j : j + 128] for j in range(0, squares.shape[1], 128))
    for i in range(squares_ref.shape[0]):
        squares_ref[i] = squares


def norm_kernel(squares_ref, hidden_ref, gain_ref, stream_ref, normed_ref):
    squares = jnp.sum(jnp.sum(squares_ref[...], axis=0), axis=1, keepdims=True)
    hidden = hidden_ref[...]
    normed = hidden * lax.rsqrt(squares / D + 1e-06) * gain_ref[...].astype(F32)
    rows_b, steps, _ = stream_ref.shape
    for b in range(rows_b):
        stream_ref[b] = hidden[b * steps : (b + 1) * steps].astype(BF16)
        normed_ref[b] = normed[b * steps : (b + 1) * steps].astype(BF16)


def call(kernel, outs, *args, flops=0):
    single = not isinstance(outs, list)
    size = sum(a.size * a.dtype.itemsize for a in args)
    vmem = pl.BlockSpec(memory_space=pltpu.VMEM)
    return pl.pallas_call(
        kernel,
        out_shape=outs,
        in_specs=[vmem] * len(args),
        out_specs=vmem if single else [vmem] * len(outs),
        compiler_params=pltpu.CompilerParams(vmem_limit_bytes=32 * 1024 * 1024),
        cost_estimate=pl.CostEstimate(flops=flops, bytes_accessed=size, transcendentals=0),
    )(*args)


def on_device(
    stream_in, queries, new_keys, new_values, key_cache, value_cache, lengths, out_weight, norm_gain
):
    rows_b, steps, width = queries.shape
    kv_heads, head_dim = key_cache.shape[2:]
    n_tp, n_far = lax.axis_size("tp"), lax.axis_size(FAR)
    n_near = lax.axis_size(NEAR)
    n_devices = n_far * n_near * n_tp
    rows = rows_b * steps
    columns = stream_in.shape[2]
    share = width // n_tp

    with jax.named_scope("weights"):
        weight = exchanged(jnp.broadcast_to(out_weight, (n_near, *out_weight.shape)), NEAR)

    with jax.named_scope("attention"):
        flat = lambda a: a.reshape(rows_b, -1, head_dim)
        parts = attend(
            queries, flat(new_keys), flat(new_values), flat(key_cache), flat(value_cache), lengths,
            jax.ShapeDtypeStruct((n_tp, rows_b + 1, 8, head_dim), BF16),
        )
        parts, weight = lax.optimization_barrier((parts, weight))
        parts = exchanged(parts, "tp")
        attended = call(combine_kernel, jax.ShapeDtypeStruct((n_far, rows, share), BF16), parts)
        attended = exchanged(attended, FAR)

    with jax.named_scope("projection"):
        projected = call(
            project_kernel, jax.ShapeDtypeStruct((n_far, rows, columns), BF16), attended, weight,
            flops=2 * n_far * rows * share * columns,
        )
        partials = exchanged(projected, "tp")
        summed = call(sum_kernel, jax.ShapeDtypeStruct((rows, columns), BF16), partials)

        def home(i):
            far, near, p = i // (n_near * n_tp), i // n_tp % n_near, i % n_tp
            return (p * n_near + near) * n_tp + far

        summed = permuted(summed, (*REP, "tp"), n_devices, home)

    with jax.named_scope("norm"):
        hidden, squares = call(
            hidden_kernel,
            [
                jax.ShapeDtypeStruct((rows, columns), F32),
                jax.ShapeDtypeStruct((n_tp, rows, 128), F32),
            ],
            summed, stream_in,
        )
        squares = exchanged(squares, "tp")
        out = jax.ShapeDtypeStruct(stream_in.shape, BF16)
        return tuple(call(norm_kernel, [out, out], squares, hidden, norm_gain.reshape(1, -1)))


def solution(mesh):
    finer = Mesh(mesh.devices.reshape(4, 4, 4, mesh.shape["tp"]), (*REP, "tp"))
    in_specs = (
        P(REP, None, "tp"),
        P(REP, None, None),
        P(REP, None, None, None),
        P(REP, None, None, None),
        P(REP, "tp", None, None),
        P(REP, "tp", None, None),
        P(REP),
        P("tp", REP),
        P("tp"),
    )
    out_specs = (P(REP, None, "tp"), P(REP, None, "tp"))
    return jax.shard_map(
        on_device, mesh=finer, in_specs=in_specs, out_specs=out_specs, check_vma=False
    )
```

```python
import math

import jax
import jax.numpy as jnp
from jax import lax
from jax.experimental import pallas as pl
from jax.experimental.pallas import tpu as pltpu
from jax.sharding import Mesh
from jax.sharding import PartitionSpec as P

D = 8192
REP = ("ra", "rb", "rc")
ARC = ("rb", "rc")
QUAD = "rc"
MASKED = -1e30
NONE_VISIBLE = -1e29
F32, BF16 = jnp.float32, jnp.bfloat16


def exchanged(pieces, axes):
    return lax.all_to_all(pieces, axes, split_axis=0, concat_axis=0, tiled=True)


def permuted(array, axes, count, target):
    return lax.ppermute(array, axes, [(i, target(i)) for i in range(count)])


def dot_rows(a, b):
    return lax.dot_general(a, b, (((1,), (1,)), ((), ())), preferred_element_type=F32)


def stacked(pieces, axis=0):
    return jnp.concatenate(pieces, axis=axis)


def attend_kernel(len_ref, q_ref, nk_ref, nv_ref, k_ref, v_ref, out_ref, stats_ref):
    b = pl.program_id(0)
    rows_b = pl.num_programs(0)
    _, steps, width = q_ref.shape
    head_dim = k_ref.shape[2]
    kv_heads = nk_ref.shape[1] // steps
    heads = width // head_dim
    rows = heads * steps
    columns = k_ref.shape[1]
    block_len = columns // kv_heads
    to_log2 = math.log2(math.e) / math.sqrt(head_dim)
    tp = lax.axis_index("tp")

    def own_head(count):
        row = lax.broadcasted_iota(jnp.int32, (rows, count), 0)
        column = lax.broadcasted_iota(jnp.int32, (rows, count), 1)
        same = (column % kv_heads) == (row // (rows // kv_heads))
        return row, column // kv_heads, same

    def masked(key_ref, visible):
        return jnp.where(visible, dot_rows(q, key_ref[0]) * to_log2, MASKED)

    _, position, same = own_head(columns)
    visible = same & (position < len_ref[b] - tp * block_len)
    row, fresh_at, same = own_head(nk_ref.shape[1])
    fresh_visible = same & (fresh_at <= row % steps) & (tp == 0)
    wide = q_ref[0].astype(F32)
    q = stacked([wide[:, h * head_dim : (h + 1) * head_dim] for h in range(heads)]).astype(BF16)
    scores, fresh = masked(k_ref, visible), masked(nk_ref, fresh_visible)
    top = jnp.maximum(scores.max(1, keepdims=True), fresh.max(1, keepdims=True))
    shift = jnp.maximum(top, NONE_VISIBLE).astype(BF16).astype(F32)
    weights, fresh_weights = jnp.exp2(scores - shift), jnp.exp2(fresh - shift)
    total = weights.sum(1, keepdims=True) + fresh_weights.sum(1, keepdims=True)
    numerator = jnp.dot(weights.astype(BF16), v_ref[0], preferred_element_type=F32)
    numerator += jnp.dot(fresh_weights.astype(BF16), nv_ref[0], preferred_element_type=F32)
    out_ref[:, b] = numerator.astype(BF16).reshape(-1, 8, head_dim)
    high = total.astype(BF16).astype(F32)
    lane = lax.broadcasted_iota(jnp.int32, (rows, head_dim), 1)
    stats = jnp.where(b == 0, jnp.zeros((rows, head_dim), F32), stats_ref[...])
    stats = jnp.where(lane == 3 * b, shift, stats)
    stats = jnp.where(lane == 3 * b + 1, high, stats)
    stats = jnp.where(lane == 3 * b + 2, total - high, stats)
    stats_ref[...] = stats
    out_ref[:, rows_b] = stats.astype(BF16).reshape(-1, 8, head_dim)


def attend(queries, new_keys, new_values, keys, values, lengths, outs):
    def of_row(a):
        return pl.BlockSpec((1, *a.shape[1:]), lambda b: (b, 0, 0))

    return pl.pallas_call(
        attend_kernel,
        grid=(queries.shape[0],),
        out_shape=outs,
        in_specs=[
            pl.BlockSpec(memory_space=pltpu.SMEM),
            *(of_row(a) for a in (queries, new_keys, new_values, keys, values)),
        ],
        out_specs=pl.BlockSpec(outs.shape, lambda b: (0, 0, 0, 0)),
        scratch_shapes=[pltpu.VMEM((outs.shape[0] * outs.shape[2], outs.shape[3]), F32)],
        compiler_params=pltpu.CompilerParams(vmem_limit_bytes=60 * 1024 * 1024),
        cost_estimate=pl.CostEstimate(
            flops=300_000_000, bytes_accessed=2 * keys.size * 2, transcendentals=600_000
        ),
    )(lengths, queries, new_keys, new_values, keys, values)


def combine_kernel(parts_ref, out_ref):
    rows_b = parts_ref.shape[1] - 1
    half = parts_ref.shape[2] // 2
    stats = parts_ref[:, rows_b].astype(F32)
    first, second = [], []
    for b in range(rows_b):
        shift, high, low = (stats[:, :, 3 * b + i : 3 * b + i + 1] for i in range(3))
        scale = jnp.exp2(shift - shift.max(0, keepdims=True))
        total = jnp.sum(scale * (high + low), axis=0)
        numerator = jnp.sum(scale * parts_ref[:, b].astype(F32), axis=0)
        attended = numerator / total
        first.append(attended[:half])
        second.append(attended[half:])
    attended = stacked([stacked(first), stacked(second)], 1).astype(BF16)
    for i in range(out_ref.shape[0]):
        out_ref[i] = attended


def side_by_side_kernel(blocks_ref, out_ref):
    for j in range(blocks_ref.shape[0]):
        out_ref[:, j * 128 : (j + 1) * 128] = blocks_ref[j]


def project_kernel(x_ref, w_ref, out_ref):
    x = x_ref[...].reshape(-1, x_ref.shape[2])
    projected = jnp.dot(x, w_ref[...], preferred_element_type=F32)
    out_ref[...] = projected.astype(BF16).reshape(out_ref.shape)


def sum_kernel(parts_ref, out_ref):
    out_ref[...] = jnp.sum(parts_ref[...].astype(F32), axis=0).astype(BF16)


def hidden_kernel(summed_ref, stream_ref, hidden_ref, squares_ref):
    stream = stacked([stream_ref[b].astype(F32) for b in range(stream_ref.shape[0])])
    hidden = stream + summed_ref[...].astype(F32)
    hidden_ref[...] = hidden
    squares = hidden * hidden
    squares = sum(squares[:, j : j + 128] for j in range(0, squares.shape[1], 128))
    for i in range(squares_ref.shape[0]):
        squares_ref[i] = squares


def norm_kernel(squares_ref, hidden_ref, gain_ref, stream_ref, normed_ref):
    squares = jnp.sum(jnp.sum(squares_ref[...], axis=0), axis=1, keepdims=True)
    hidden = hidden_ref[...]
    normed = hidden * lax.rsqrt(squares / D + 1e-06) * gain_ref[...].astype(F32)
    rows_b, steps, _ = stream_ref.shape
    for b in range(rows_b):
        stream_ref[b] = hidden[b * steps : (b + 1) * steps].astype(BF16)
        normed_ref[b] = normed[b * steps : (b + 1) * steps].astype(BF16)


def call(kernel, outs, *args, flops=0):
    single = not isinstance(outs, list)
    size = sum(a.size * a.dtype.itemsize for a in args)
    vmem = pl.BlockSpec(memory_space=pltpu.VMEM)
    return pl.pallas_call(
        kernel,
        out_shape=outs,
        in_specs=[vmem] * len(args),
        out_specs=vmem if single else [vmem] * len(outs),
        compiler_params=pltpu.CompilerParams(vmem_limit_bytes=32 * 1024 * 1024),
        cost_estimate=pl.CostEstimate(flops=flops, bytes_accessed=size, transcendentals=0),
    )(*args)


def on_device(
    stream_in, queries, new_keys, new_values, key_cache, value_cache, lengths, out_weight, norm_gain
):
    rows_b, steps, width = queries.shape
    kv_heads, head_dim = key_cache.shape[2:]
    n_tp, n_arc = lax.axis_size("tp"), lax.axis_size(ARC)
    n_quad = lax.axis_size(QUAD)
    n_rep = n_arc * lax.axis_size("ra")
    rows = rows_b * steps
    columns = stream_in.shape[2]
    share = width // n_tp

    with jax.named_scope("weights"):
        quad = exchanged(jnp.broadcast_to(out_weight, (n_quad, *out_weight.shape)), QUAD)

    with jax.named_scope("attention"):
        flat = lambda a: a.reshape(rows_b, -1, head_dim)
        parts = attend(
            queries, flat(new_keys), flat(new_values), flat(key_cache), flat(value_cache), lengths,
            jax.ShapeDtypeStruct((n_tp, rows_b + 1, 8, head_dim), BF16),
        )
        parts, quad = lax.optimization_barrier((parts, quad))
        weight = permuted(quad, REP, n_rep, lambda r: (r % n_quad) * n_arc + r // n_quad)
        weight = call(
            side_by_side_kernel, jax.ShapeDtypeStruct((share, columns), BF16), weight, flops=20_000_000_000
        )
        parts = exchanged(parts, "tp")
        attended = call(combine_kernel, jax.ShapeDtypeStruct((n_arc, rows, share), BF16), parts)
        attended = exchanged(attended, ARC)

    with jax.named_scope("projection"):
        projected = call(
            project_kernel, jax.ShapeDtypeStruct((n_arc, rows, columns), BF16), attended, weight,
            flops=2 * n_arc * rows * share * columns,
        )
        partials = exchanged(projected, "tp")
        summed = call(sum_kernel, jax.ShapeDtypeStruct((rows, columns), BF16), partials)

        def home(i):
            r, p = i // n_tp, i % n_tp
            return (r // n_arc * n_arc + p) * n_tp + r % n_arc

        summed = permuted(summed, (*REP, "tp"), n_rep * n_tp, home)

    with jax.named_scope("norm"):
        hidden, squares = call(
            hidden_kernel,
            [
                jax.ShapeDtypeStruct((rows, columns), F32),
                jax.ShapeDtypeStruct((n_tp, rows, 128), F32),
            ],
            summed, stream_in,
        )
        squares = exchanged(squares, "tp")
        out = jax.ShapeDtypeStruct(stream_in.shape, BF16)
        return tuple(call(norm_kernel, [out, out], squares, hidden, norm_gain.reshape(1, -1)))


def solution(mesh):
    finer = Mesh(mesh.devices.reshape(4, 4, 4, mesh.shape["tp"]), (*REP, "tp"))
    in_specs = (
        P(REP, None, "tp"),
        P(REP, None, None),
        P(REP, None, None, None),
        P(REP, None, None, None),
        P(REP, "tp", None, None),
        P(REP, "tp", None, None),
        P(REP),
        P("tp", REP),
        P("tp"),
    )
    out_specs = (P(REP, None, "tp"), P(REP, None, "tp"))
    return jax.shard_map(
        on_device, mesh=finer, in_specs=in_specs, out_specs=out_specs, check_vma=False
    )
```

```python
import math

import jax
import jax.numpy as jnp
from jax import lax
from jax.experimental import pallas as pl
from jax.experimental.pallas import tpu as pltpu
from jax.sharding import Mesh
from jax.sharding import PartitionSpec as P

D = 8192
REP = ("ra", "rb", "rc")
ARC = ("rb", "rc")
QUAD = "rc"
MASKED = -1e30
NONE_VISIBLE = -1e29
F32, BF16 = jnp.float32, jnp.bfloat16


def exchanged(pieces, axes):
    return lax.all_to_all(pieces, axes, split_axis=0, concat_axis=0, tiled=True)


def permuted(array, target):
    axes = (*REP, "tp")
    return lax.ppermute(array, axes, [(i, target(i)) for i in range(lax.axis_size(axes))])


def dot_rows(a, b):
    return lax.dot_general(a, b, (((1,), (1,)), ((), ())), preferred_element_type=F32)


def stacked(pieces, axis=0):
    return jnp.concatenate(pieces, axis=axis)


def attend_kernel(len_ref, q_ref, nk_ref, nv_ref, k_ref, v_ref, out_ref, stats_ref):
    b = pl.program_id(0)
    rows_b = pl.num_programs(0)
    _, steps, width = q_ref.shape
    head_dim = k_ref.shape[2]
    kv_heads = nk_ref.shape[1] // steps
    heads = width // head_dim
    rows = heads * steps
    columns = k_ref.shape[1]
    block_len = columns // kv_heads
    to_log2 = math.log2(math.e) / math.sqrt(head_dim)
    tp = lax.axis_index("tp")

    def own_head(count):
        row = lax.broadcasted_iota(jnp.int32, (rows, count), 0)
        column = lax.broadcasted_iota(jnp.int32, (rows, count), 1)
        same = (column % kv_heads) == (row // (rows // kv_heads))
        return row, column // kv_heads, same

    def masked(key_ref, visible):
        return jnp.where(visible, dot_rows(q, key_ref[0]) * to_log2, MASKED)

    _, position, same = own_head(columns)
    visible = same & (position < len_ref[b] - tp * block_len)
    row, fresh_at, same = own_head(nk_ref.shape[1])
    fresh_visible = same & (fresh_at <= row % steps) & (tp == 0)
    wide = q_ref[0].astype(F32)
    q = stacked([wide[:, h * head_dim : (h + 1) * head_dim] for h in range(heads)]).astype(BF16)
    scores, fresh = masked(k_ref, visible), masked(nk_ref, fresh_visible)
    top = jnp.maximum(scores.max(1, keepdims=True), fresh.max(1, keepdims=True))
    shift = jnp.maximum(top, NONE_VISIBLE).astype(BF16).astype(F32)
    weights, fresh_weights = jnp.exp2(scores - shift), jnp.exp2(fresh - shift)
    total = weights.sum(1, keepdims=True) + fresh_weights.sum(1, keepdims=True)
    numerator = jnp.dot(weights.astype(BF16), v_ref[0], preferred_element_type=F32)
    numerator += jnp.dot(fresh_weights.astype(BF16), nv_ref[0], preferred_element_type=F32)
    out_ref[:, b] = numerator.astype(BF16).reshape(-1, 8, head_dim)
    high = total.astype(BF16).astype(F32)
    lane = lax.broadcasted_iota(jnp.int32, (rows, head_dim), 1)
    stats = jnp.where(b == 0, jnp.zeros((rows, head_dim), F32), stats_ref[...])
    stats = jnp.where(lane == 3 * b, shift, stats)
    stats = jnp.where(lane == 3 * b + 1, high, stats)
    stats = jnp.where(lane == 3 * b + 2, total - high, stats)
    stats_ref[...] = stats
    out_ref[:, rows_b] = stats.astype(BF16).reshape(-1, 8, head_dim)


def attend(queries, new_keys, new_values, keys, values, lengths, outs):
    def of_row(a):
        return pl.BlockSpec((1, *a.shape[1:]), lambda b: (b, 0, 0))

    return pl.pallas_call(
        attend_kernel,
        grid=(queries.shape[0],),
        out_shape=outs,
        in_specs=[
            pl.BlockSpec(memory_space=pltpu.SMEM),
            *(of_row(a) for a in (queries, new_keys, new_values, keys, values)),
        ],
        out_specs=pl.BlockSpec(outs.shape, lambda b: (0, 0, 0, 0)),
        scratch_shapes=[pltpu.VMEM((outs.shape[0] * outs.shape[2], outs.shape[3]), F32)],
        compiler_params=pltpu.CompilerParams(vmem_limit_bytes=60 * 1024 * 1024),
        cost_estimate=pl.CostEstimate(
            flops=300_000_000, bytes_accessed=2 * keys.size * 2, transcendentals=600_000
        ),
    )(lengths, queries, new_keys, new_values, keys, values)


def combine_kernel(parts_ref, out_ref):
    rows_b = parts_ref.shape[1] - 1
    half = parts_ref.shape[2] // 2
    stats = parts_ref[:, rows_b].astype(F32)
    first, second = [], []
    for b in range(rows_b):
        shift, high, low = (stats[:, :, 3 * b + i : 3 * b + i + 1] for i in range(3))
        scale = jnp.exp2(shift - shift.max(0, keepdims=True))
        total = jnp.sum(scale * (high + low), axis=0)
        numerator = jnp.sum(scale * parts_ref[:, b].astype(F32), axis=0)
        attended = numerator / total
        first.append(attended[:half])
        second.append(attended[half:])
    out_ref[...] = stacked([stacked(first), stacked(second)], 1).astype(BF16)


def copies_kernel(in_ref, out_ref):
    for i in range(out_ref.shape[0]):
        out_ref[i] = in_ref[...]


def side_by_side_kernel(blocks_ref, out_ref):
    for j in range(blocks_ref.shape[0]):
        out_ref[:, j * 128 : (j + 1) * 128] = blocks_ref[j]


def project_kernel(x_ref, w_ref, out_ref):
    x = x_ref[...].reshape(-1, x_ref.shape[2])
    projected = jnp.dot(x, w_ref[...], preferred_element_type=F32)
    out_ref[...] = projected.astype(BF16).reshape(out_ref.shape)


def hidden_kernel(partials_ref, stream_ref, hidden_ref, squares_ref):
    stream = stacked([stream_ref[b].astype(F32) for b in range(stream_ref.shape[0])])
    hidden = stream + jnp.sum(partials_ref[...].astype(F32), axis=0)
    hidden_ref[...] = hidden
    squares = hidden * hidden
    squares = sum(squares[:, j : j + 128] for j in range(0, squares.shape[1], 128))
    for i in range(squares_ref.shape[0]):
        squares_ref[i] = squares


def norm_kernel(squares_ref, hidden_ref, gain_ref, stream_ref, normed_ref):
    squares = jnp.sum(jnp.sum(squares_ref[...], axis=0), axis=1, keepdims=True)
    hidden = hidden_ref[...]
    normed = hidden * lax.rsqrt(squares / D + 1e-06) * gain_ref[...].astype(F32)
    rows_b, steps, _ = stream_ref.shape
    for b in range(rows_b):
        stream_ref[b] = hidden[b * steps : (b + 1) * steps].astype(BF16)
        normed_ref[b] = normed[b * steps : (b + 1) * steps].astype(BF16)


def call(kernel, outs, *args, flops=0):
    single = not isinstance(outs, list)
    size = sum(a.size * a.dtype.itemsize for a in args)
    vmem = pl.BlockSpec(memory_space=pltpu.VMEM)
    return pl.pallas_call(
        kernel,
        out_shape=outs,
        in_specs=[vmem] * len(args),
        out_specs=vmem if single else [vmem] * len(outs),
        compiler_params=pltpu.CompilerParams(vmem_limit_bytes=32 * 1024 * 1024),
        cost_estimate=pl.CostEstimate(flops=flops, bytes_accessed=size, transcendentals=0),
    )(*args)


def on_device(
    stream_in, queries, new_keys, new_values, key_cache, value_cache, lengths, out_weight, norm_gain
):
    rows_b, steps, width = queries.shape
    kv_heads, head_dim = key_cache.shape[2:]
    n_tp, n_arc = lax.axis_size("tp"), lax.axis_size(ARC)
    n_quad = lax.axis_size(QUAD)
    rows = rows_b * steps
    columns = stream_in.shape[2]
    share = width // n_tp

    def swapped(i):
        arc, place, p = i // (n_arc * n_tp), i // n_tp % n_arc, i % n_tp
        return (arc * n_arc + p) * n_tp + place

    def weight_home(i):
        quad, arc, p = i // (n_quad * n_tp), i // n_tp % n_quad, i % n_tp
        return (arc * n_arc + p) * n_tp + quad

    with jax.named_scope("weights"):
        quad = exchanged(jnp.broadcast_to(out_weight, (n_quad, *out_weight.shape)), QUAD)

    with jax.named_scope("attention"):
        flat = lambda a: a.reshape(rows_b, -1, head_dim)
        parts = attend(
            queries, flat(new_keys), flat(new_values), flat(key_cache), flat(value_cache), lengths,
            jax.ShapeDtypeStruct((n_tp, rows_b + 1, 8, head_dim), BF16),
        )
        parts, quad = lax.optimization_barrier((parts, quad))
        weight = permuted(quad, weight_home)
        weight = call(
            side_by_side_kernel, jax.ShapeDtypeStruct((share, columns), BF16), weight, flops=20_000_000_000
        )
        parts = exchanged(parts, "tp")
        attended = call(combine_kernel, jax.ShapeDtypeStruct((rows, share), BF16), parts)
        attended = permuted(attended, swapped)
        attended = call(
            copies_kernel, jax.ShapeDtypeStruct((n_tp, rows, share), BF16), attended
        )
        attended = exchanged(attended, "tp")

    with jax.named_scope("projection"):
        projected = call(
            project_kernel, jax.ShapeDtypeStruct((n_arc, rows, columns), BF16), attended, weight,
            flops=2 * n_arc * rows * share * columns,
        )
        partials = exchanged(projected, ARC)

    with jax.named_scope("norm"):
        hidden, squares = call(
            hidden_kernel,
            [
                jax.ShapeDtypeStruct((rows, columns), F32),
                jax.ShapeDtypeStruct((n_tp, rows, 128), F32),
            ],
            partials, stream_in,
        )
        squares = exchanged(squares, "tp")
        out = jax.ShapeDtypeStruct(stream_in.shape, BF16)
        return tuple(call(norm_kernel, [out, out], squares, hidden, norm_gain.reshape(1, -1)))


def solution(mesh):
    finer = Mesh(mesh.devices.reshape(4, 4, 4, mesh.shape["tp"]), (*REP, "tp"))
    in_specs = (
        P(REP, None, "tp"),
        P(REP, None, None),
        P(REP, None, None, None),
        P(REP, None, None, None),
        P(REP, "tp", None, None),
        P(REP, "tp", None, None),
        P(REP),
        P("tp", REP),
        P("tp"),
    )
    out_specs = (P(REP, None, "tp"), P(REP, None, "tp"))
    return jax.shard_map(
        on_device, mesh=finer, in_specs=in_specs, out_specs=out_specs, check_vma=False
    )
```

```python
import math

import jax
import jax.numpy as jnp
from jax import lax
from jax.experimental import pallas as pl
from jax.experimental.pallas import tpu as pltpu
from jax.sharding import Mesh
from jax.sharding import PartitionSpec as P

D = 8192
REP = ("ra", "rb", "rc")
ARC = ("rb", "rc")
QUAD = "rc"
MASKED = -1e30
NONE_VISIBLE = -1e29
F32, BF16 = jnp.float32, jnp.bfloat16


def exchanged(pieces, axes):
    return lax.all_to_all(pieces, axes, split_axis=0, concat_axis=0, tiled=True)


def permuted(array, axes, count, target):
    return lax.ppermute(array, axes, [(i, target(i)) for i in range(count)])


def dot_rows(a, b):
    return lax.dot_general(a, b, (((1,), (1,)), ((), ())), preferred_element_type=F32)


def stacked(pieces, axis=0):
    return jnp.concatenate(pieces, axis=axis)


def copies_kernel(in_ref, out_ref, sems):
    sends = [
        pltpu.make_async_copy(in_ref, out_ref.at[i], sems.at[i]) for i in range(out_ref.shape[0])
    ]
    for send in sends:
        send.start()
    for send in sends:
        send.wait()


def copies(array, count):
    return pl.pallas_call(
        copies_kernel,
        out_shape=jax.ShapeDtypeStruct((count, *array.shape), array.dtype),
        in_specs=[pl.BlockSpec(memory_space=pl.ANY)],
        out_specs=pl.BlockSpec(memory_space=pl.ANY),
        scratch_shapes=[pltpu.SemaphoreType.DMA((count,))],
        compiler_params=pltpu.CompilerParams(vmem_limit_bytes=60 * 1024 * 1024),
    )(array)


def attend_kernel(len_ref, q_ref, nk_ref, nv_ref, k_ref, v_ref, out_ref, stats_ref):
    b = pl.program_id(0)
    rows_b = pl.num_programs(0)
    _, steps, width = q_ref.shape
    head_dim = k_ref.shape[2]
    kv_heads = nk_ref.shape[1] // steps
    heads = width // head_dim
    rows = heads * steps
    columns = k_ref.shape[1]
    block_len = columns // kv_heads
    to_log2 = math.log2(math.e) / math.sqrt(head_dim)
    tp = lax.axis_index("tp")

    def masked(key_ref, limit):
        count = key_ref.shape[1]
        head = lax.broadcasted_iota(jnp.int32, (kv_heads, 1, count), 0)
        column = lax.broadcasted_iota(jnp.int32, (kv_heads, 1, count), 2)
        visible = (column % kv_heads == head) & (column // kv_heads < limit)
        bias = jnp.where(visible, 0.0, MASKED)
        scores = (dot_rows(q, key_ref[0]) * to_log2).reshape(kv_heads, -1, count)
        return (scores + bias).reshape(rows, count)

    wide = q_ref[0].astype(F32)
    q = stacked([wide[:, h * head_dim : (h + 1) * head_dim] for h in range(heads)]).astype(BF16)
    scores = masked(k_ref, len_ref[b] - tp * block_len)
    step = lax.broadcasted_iota(jnp.int32, (1, rows // kv_heads, 1), 1) % steps
    fresh = masked(nk_ref, jnp.where(tp == 0, step + 1, 0))
    top = jnp.maximum(scores.max(1, keepdims=True), fresh.max(1, keepdims=True))
    shift = jnp.maximum(top, NONE_VISIBLE).astype(BF16).astype(F32)
    weights, fresh_weights = jnp.exp2(scores - shift), jnp.exp2(fresh - shift)
    total = weights.sum(1, keepdims=True) + fresh_weights.sum(1, keepdims=True)
    numerator = jnp.dot(weights.astype(BF16), v_ref[0], preferred_element_type=F32)
    numerator += jnp.dot(fresh_weights.astype(BF16), nv_ref[0], preferred_element_type=F32)
    out_ref[:, b] = numerator.astype(BF16).reshape(-1, 8, head_dim)
    high = total.astype(BF16).astype(F32)
    lane = lax.broadcasted_iota(jnp.int32, (rows, head_dim), 1)
    stats = jnp.where(b == 0, jnp.zeros((rows, head_dim), F32), stats_ref[...])
    stats = jnp.where(lane == 3 * b, shift, stats)
    stats = jnp.where(lane == 3 * b + 1, high, stats)
    stats = jnp.where(lane == 3 * b + 2, total - high, stats)
    stats_ref[...] = stats
    out_ref[:, rows_b] = stats.astype(BF16).reshape(-1, 8, head_dim)


def attend(queries, new_keys, new_values, keys, values, lengths, outs):
    def of_row(a):
        return pl.BlockSpec((1, *a.shape[1:]), lambda b: (b, 0, 0))

    return pl.pallas_call(
        attend_kernel,
        grid=(queries.shape[0],),
        out_shape=outs,
        in_specs=[
            pl.BlockSpec(memory_space=pltpu.SMEM),
            *(of_row(a) for a in (queries, new_keys, new_values, keys, values)),
        ],
        out_specs=pl.BlockSpec(outs.shape, lambda b: (0, 0, 0, 0)),
        scratch_shapes=[pltpu.VMEM((outs.shape[0] * outs.shape[2], outs.shape[3]), F32)],
        compiler_params=pltpu.CompilerParams(vmem_limit_bytes=60 * 1024 * 1024),
        cost_estimate=pl.CostEstimate(
            flops=300_000_000, bytes_accessed=2 * keys.size * 2, transcendentals=600_000
        ),
    )(lengths, queries, new_keys, new_values, keys, values)


def combine_kernel(parts_ref, out_ref):
    rows_b = parts_ref.shape[1] - 1
    half = parts_ref.shape[2] // 2
    stats = parts_ref[:, rows_b].astype(F32)
    first, second = [], []
    for b in range(rows_b):
        shift, high, low = (stats[:, :, 3 * b + i : 3 * b + i + 1] for i in range(3))
        scale = jnp.exp2(shift - shift.max(0, keepdims=True))
        total = jnp.sum(scale * (high + low), axis=0)
        numerator = jnp.sum(scale * parts_ref[:, b].astype(F32), axis=0)
        attended = numerator / total
        first.append(attended[:half])
        second.append(attended[half:])
    attended = stacked([stacked(first), stacked(second)], 1).astype(BF16)
    for i in range(out_ref.shape[0]):
        out_ref[i] = attended


def side_by_side_kernel(blocks_ref, out_ref):
    for j in range(blocks_ref.shape[0]):
        out_ref[:, j * 128 : (j + 1) * 128] = blocks_ref[j]


def project_kernel(x_ref, w_ref, out_ref):
    x = x_ref[...].reshape(-1, x_ref.shape[2])
    projected = jnp.dot(x, w_ref[...], preferred_element_type=F32)
    out_ref[...] = projected.astype(BF16).reshape(out_ref.shape)


def sum_kernel(parts_ref, out_ref):
    out_ref[...] = jnp.sum(parts_ref[...].astype(F32), axis=0).astype(BF16)


def hidden_kernel(summed_ref, stream_ref, hidden_ref, squares_ref):
    stream = stacked([stream_ref[b].astype(F32) for b in range(stream_ref.shape[0])])
    hidden = stream + summed_ref[...].astype(F32)
    hidden_ref[...] = hidden
    squares = hidden * hidden
    squares = sum(squares[:, j : j + 128] for j in range(0, squares.shape[1], 128))
    for i in range(squares_ref.shape[0]):
        squares_ref[i] = squares


def norm_kernel(squares_ref, hidden_ref, gain_ref, stream_ref, normed_ref):
    squares = jnp.sum(jnp.sum(squares_ref[...], axis=0), axis=1, keepdims=True)
    hidden = hidden_ref[...]
    normed = hidden * lax.rsqrt(squares / D + 1e-06) * gain_ref[...].astype(F32)
    rows_b, steps, _ = stream_ref.shape
    for b in range(rows_b):
        stream_ref[b] = hidden[b * steps : (b + 1) * steps].astype(BF16)
        normed_ref[b] = normed[b * steps : (b + 1) * steps].astype(BF16)


def call(kernel, outs, *args, flops=0):
    single = not isinstance(outs, list)
    size = sum(a.size * a.dtype.itemsize for a in args)
    vmem = pl.BlockSpec(memory_space=pltpu.VMEM)
    return pl.pallas_call(
        kernel,
        out_shape=outs,
        in_specs=[vmem] * len(args),
        out_specs=vmem if single else [vmem] * len(outs),
        compiler_params=pltpu.CompilerParams(vmem_limit_bytes=32 * 1024 * 1024),
        cost_estimate=pl.CostEstimate(flops=flops, bytes_accessed=size, transcendentals=0),
    )(*args)


def on_device(
    stream_in, queries, new_keys, new_values, key_cache, value_cache, lengths, out_weight, norm_gain
):
    rows_b, steps, width = queries.shape
    kv_heads, head_dim = key_cache.shape[2:]
    n_tp, n_arc = lax.axis_size("tp"), lax.axis_size(ARC)
    n_quad = lax.axis_size(QUAD)
    n_rep = n_arc * lax.axis_size("ra")
    rows = rows_b * steps
    columns = stream_in.shape[2]
    share = width // n_tp

    with jax.named_scope("weights"):
        quad = exchanged(copies(out_weight, n_quad), QUAD)
        lengths, quad = lax.optimization_barrier((lengths, quad))
        weight = permuted(quad, REP, n_rep, lambda r: (r % n_quad) * n_arc + r // n_quad)
        weight = call(
            side_by_side_kernel, jax.ShapeDtypeStruct((share, columns), BF16), weight, flops=20_000_000_000
        )

    with jax.named_scope("attention"):
        flat = lambda a: a.reshape(rows_b, -1, head_dim)
        parts = attend(
            queries, flat(new_keys), flat(new_values), flat(key_cache), flat(value_cache), lengths,
            jax.ShapeDtypeStruct((n_tp, rows_b + 1, 8, head_dim), BF16),
        )
        parts = exchanged(parts, "tp")
        attended = call(combine_kernel, jax.ShapeDtypeStruct((n_arc, rows, share), BF16), parts)
        attended = exchanged(attended, ARC)

    with jax.named_scope("projection"):
        projected = call(
            project_kernel, jax.ShapeDtypeStruct((n_arc, rows, columns), BF16), attended, weight,
            flops=2 * n_arc * rows * share * columns,
        )
        partials = exchanged(projected, "tp")
        summed = call(sum_kernel, jax.ShapeDtypeStruct((rows, columns), BF16), partials)

        def home(i):
            r, p = i // n_tp, i % n_tp
            return (r // n_arc * n_arc + p) * n_tp + r % n_arc

        summed = permuted(summed, (*REP, "tp"), n_rep * n_tp, home)

    with jax.named_scope("norm"):
        hidden, squares = call(
            hidden_kernel,
            [
                jax.ShapeDtypeStruct((rows, columns), F32),
                jax.ShapeDtypeStruct((n_tp, rows, 128), F32),
            ],
            summed, stream_in,
        )
        squares = exchanged(squares, "tp")
        out = jax.ShapeDtypeStruct(stream_in.shape, BF16)
        return tuple(call(norm_kernel, [out, out], squares, hidden, norm_gain.reshape(1, -1)))


def solution(mesh):
    finer = Mesh(mesh.devices.reshape(4, 4, 4, mesh.shape["tp"]), (*REP, "tp"))
    in_specs = (
        P(REP, None, "tp"),
        P(REP, None, None),
        P(REP, None, None, None),
        P(REP, None, None, None),
        P(REP, "tp", None, None),
        P(REP, "tp", None, None),
        P(REP),
        P("tp", REP),
        P("tp"),
    )
    out_specs = (P(REP, None, "tp"), P(REP, None, "tp"))
    return jax.shard_map(
        on_device, mesh=finer, in_specs=in_specs, out_specs=out_specs, check_vma=False
    )
```

```python
import math

import jax
import jax.numpy as jnp
from jax import lax
from jax.experimental import pallas as pl
from jax.experimental.pallas import tpu as pltpu
from jax.sharding import Mesh
from jax.sharding import PartitionSpec as P

D = 8192
REP = ("ra", "rb", "rc")
ARC = ("rb", "rc")
QUAD = "rc"
MASKED = -1e30
NONE_VISIBLE = -1e29
F32, BF16 = jnp.float32, jnp.bfloat16


def exchanged(pieces, axes):
    return lax.all_to_all(pieces, axes, split_axis=0, concat_axis=0, tiled=True)


def permuted(array, axes, count, target):
    return lax.ppermute(array, axes, [(i, target(i)) for i in range(count)])


def dot_rows(a, b):
    return lax.dot_general(a, b, (((1,), (1,)), ((), ())), preferred_element_type=F32)


def stacked(pieces, axis=0):
    return jnp.concatenate(pieces, axis=axis)


def attend_kernel(len_ref, q_ref, nk_ref, nv_ref, k_ref, v_ref, out_ref, stats_ref):
    b = pl.program_id(0)
    rows_b = pl.num_programs(0)
    _, steps, width = q_ref.shape
    head_dim = k_ref.shape[2]
    kv_heads = nk_ref.shape[1] // steps
    heads = width // head_dim
    rows = heads * steps
    columns = k_ref.shape[1]
    block_len = columns // kv_heads
    to_log2 = math.log2(math.e) / math.sqrt(head_dim)
    tp = lax.axis_index("tp")

    def own_head(count):
        row = lax.broadcasted_iota(jnp.int32, (rows, count), 0)
        column = lax.broadcasted_iota(jnp.int32, (rows, count), 1)
        same = (column % kv_heads) == (row // (rows // kv_heads))
        return row, column // kv_heads, same

    def masked(key_ref, visible):
        return jnp.where(visible, dot_rows(q, key_ref[0]) * to_log2, MASKED)

    _, position, same = own_head(columns)
    visible = same & (position < len_ref[b] - tp * block_len)
    row, fresh_at, same = own_head(nk_ref.shape[1])
    fresh_visible = same & (fresh_at <= row % steps) & (tp == 0)
    wide = q_ref[0].astype(F32)
    q = stacked([wide[:, h * head_dim : (h + 1) * head_dim] for h in range(heads)]).astype(BF16)
    scores, fresh = masked(k_ref, visible), masked(nk_ref, fresh_visible)
    top = jnp.maximum(scores.max(1, keepdims=True), fresh.max(1, keepdims=True))
    shift = jnp.maximum(top, NONE_VISIBLE).astype(BF16).astype(F32)
    weights, fresh_weights = jnp.exp2(scores - shift), jnp.exp2(fresh - shift)
    total = weights.sum(1, keepdims=True) + fresh_weights.sum(1, keepdims=True)
    numerator = jnp.dot(weights.astype(BF16), v_ref[0], preferred_element_type=F32)
    numerator += jnp.dot(fresh_weights.astype(BF16), nv_ref[0], preferred_element_type=F32)
    out_ref[:, b] = numerator.astype(BF16).reshape(-1, 8, head_dim)
    high = total.astype(BF16).astype(F32)
    lane = lax.broadcasted_iota(jnp.int32, (rows, head_dim), 1)
    stats = jnp.where(b == 0, jnp.zeros((rows, head_dim), F32), stats_ref[...])
    stats = jnp.where(lane == 3 * b, shift, stats)
    stats = jnp.where(lane == 3 * b + 1, high, stats)
    stats = jnp.where(lane == 3 * b + 2, total - high, stats)
    stats_ref[...] = stats
    out_ref[:, rows_b] = stats.astype(BF16).reshape(-1, 8, head_dim)


def attend(queries, new_keys, new_values, keys, values, lengths, outs):
    def of_row(a):
        return pl.BlockSpec((1, *a.shape[1:]), lambda b: (b, 0, 0))

    return pl.pallas_call(
        attend_kernel,
        grid=(queries.shape[0],),
        out_shape=outs,
        in_specs=[
            pl.BlockSpec(memory_space=pltpu.SMEM),
            *(of_row(a) for a in (queries, new_keys, new_values, keys, values)),
        ],
        out_specs=pl.BlockSpec(outs.shape, lambda b: (0, 0, 0, 0)),
        scratch_shapes=[pltpu.VMEM((outs.shape[0] * outs.shape[2], outs.shape[3]), F32)],
        compiler_params=pltpu.CompilerParams(vmem_limit_bytes=60 * 1024 * 1024),
        cost_estimate=pl.CostEstimate(
            flops=300_000_000, bytes_accessed=2 * keys.size * 2, transcendentals=600_000
        ),
    )(lengths, queries, new_keys, new_values, keys, values)


def combine_kernel(parts_ref, out_ref):
    rows_b = parts_ref.shape[1] - 1
    half = parts_ref.shape[2] // 2
    stats = parts_ref[:, rows_b].astype(F32)
    first, second = [], []
    for b in range(rows_b):
        shift, high, low = (stats[:, :, 3 * b + i : 3 * b + i + 1] for i in range(3))
        scale = jnp.exp2(shift - shift.max(0, keepdims=True))
        total = jnp.sum(scale * (high + low), axis=0)
        numerator = jnp.sum(scale * parts_ref[:, b].astype(F32), axis=0)
        attended = numerator / total
        first.append(attended[:half])
        second.append(attended[half:])
    attended = stacked([stacked(first), stacked(second)], 1).astype(BF16)
    for i in range(out_ref.shape[0]):
        out_ref[i] = attended


def side_by_side_kernel(blocks_ref, out_ref):
    for j in range(blocks_ref.shape[0]):
        out_ref[:, j * 128 : (j + 1) * 128] = blocks_ref[j]


def project_kernel(x_ref, w_ref, out_ref):
    x = x_ref[...].reshape(-1, x_ref.shape[2])
    projected = jnp.dot(x, w_ref[...], preferred_element_type=F32)
    out_ref[...] = projected.astype(BF16).reshape(out_ref.shape)


def sum_kernel(parts_ref, out_ref):
    out_ref[...] = jnp.sum(parts_ref[...].astype(F32), axis=0).astype(BF16)


def hidden_kernel(summed_ref, stream_ref, hidden_ref, squares_ref):
    stream = stacked([stream_ref[b].astype(F32) for b in range(stream_ref.shape[0])])
    hidden = stream + summed_ref[...].astype(F32)
    hidden_ref[...] = hidden
    squares = hidden * hidden
    squares = sum(squares[:, j : j + 128] for j in range(0, squares.shape[1], 128))
    for i in range(squares_ref.shape[0]):
        squares_ref[i] = squares


def norm_kernel(squares_ref, hidden_ref, gain_ref, stream_ref, normed_ref):
    squares = jnp.sum(jnp.sum(squares_ref[...], axis=0), axis=1, keepdims=True)
    hidden = hidden_ref[...]
    normed = hidden * lax.rsqrt(squares / D + 1e-06) * gain_ref[...].astype(F32)
    rows_b, steps, _ = stream_ref.shape
    for b in range(rows_b):
        stream_ref[b] = hidden[b * steps : (b + 1) * steps].astype(BF16)
        normed_ref[b] = normed[b * steps : (b + 1) * steps].astype(BF16)


def call(kernel, outs, *args, flops=0):
    single = not isinstance(outs, list)
    size = sum(a.size * a.dtype.itemsize for a in args)
    vmem = pl.BlockSpec(memory_space=pltpu.VMEM)
    return pl.pallas_call(
        kernel,
        out_shape=outs,
        in_specs=[vmem] * len(args),
        out_specs=vmem if single else [vmem] * len(outs),
        compiler_params=pltpu.CompilerParams(vmem_limit_bytes=32 * 1024 * 1024),
        cost_estimate=pl.CostEstimate(flops=flops, bytes_accessed=size, transcendentals=0),
    )(*args)


def on_device(
    stream_in, queries, new_keys, new_values, key_cache, value_cache, lengths, out_weight, norm_gain
):
    rows_b, steps, width = queries.shape
    kv_heads, head_dim = key_cache.shape[2:]
    n_tp, n_arc = lax.axis_size("tp"), lax.axis_size(ARC)
    n_quad = lax.axis_size(QUAD)
    n_rep = n_arc * lax.axis_size("ra")
    rows = rows_b * steps
    columns = stream_in.shape[2]
    share = width // n_tp

    with jax.named_scope("weights"):
        quad = exchanged(jnp.broadcast_to(out_weight, (n_quad, *out_weight.shape)), QUAD)

    with jax.named_scope("attention"):
        flat = lambda a: a.reshape(rows_b, -1, head_dim)
        parts = attend(
            queries, flat(new_keys), flat(new_values), flat(key_cache), flat(value_cache), lengths,
            jax.ShapeDtypeStruct((n_tp, rows_b + 1, 8, head_dim), BF16),
        )
        parts, quad = lax.optimization_barrier((parts, quad))
        weight = permuted(quad, REP, n_rep, lambda r: (r % n_quad) * n_arc + r // n_quad)
        weight = call(
            side_by_side_kernel, jax.ShapeDtypeStruct((share, columns), BF16), weight, flops=20_000_000_000
        )
        parts = exchanged(parts, "tp")
        attended = call(combine_kernel, jax.ShapeDtypeStruct((n_arc, rows, share), BF16), parts, flops=4_000_000_000)
        attended = exchanged(attended, ARC)

    with jax.named_scope("projection"):
        projected = call(
            project_kernel, jax.ShapeDtypeStruct((n_arc, rows, columns), BF16), attended, weight,
            flops=2 * n_arc * rows * share * columns,
        )
        partials = exchanged(projected, "tp")
        summed = call(sum_kernel, jax.ShapeDtypeStruct((rows, columns), BF16), partials)

        def home(i):
            r, p = i // n_tp, i % n_tp
            return (r // n_arc * n_arc + p) * n_tp + r % n_arc

        summed = permuted(summed, (*REP, "tp"), n_rep * n_tp, home)

    with jax.named_scope("norm"):
        hidden, squares = call(
            hidden_kernel,
            [
                jax.ShapeDtypeStruct((rows, columns), F32),
                jax.ShapeDtypeStruct((n_tp, rows, 128), F32),
            ],
            summed, stream_in,
        )
        squares = exchanged(squares, "tp")
        out = jax.ShapeDtypeStruct(stream_in.shape, BF16)
        return tuple(call(norm_kernel, [out, out], squares, hidden, norm_gain.reshape(1, -1)))


def solution(mesh):
    finer = Mesh(mesh.devices.reshape(4, 4, 4, mesh.shape["tp"]), (*REP, "tp"))
    in_specs = (
        P(REP, None, "tp"),
        P(REP, None, None),
        P(REP, None, None, None),
        P(REP, None, None, None),
        P(REP, "tp", None, None),
        P(REP, "tp", None, None),
        P(REP),
        P("tp", REP),
        P("tp"),
    )
    out_specs = (P(REP, None, "tp"), P(REP, None, "tp"))
    return jax.shard_map(
        on_device, mesh=finer, in_specs=in_specs, out_specs=out_specs, check_vma=False
    )
```

```python
import functools
import math

import jax
import jax.numpy as jnp
from jax import lax
from jax.experimental import pallas as pl
from jax.experimental.pallas import tpu as pltpu
from jax.sharding import Mesh
from jax.sharding import PartitionSpec as P

D = 8192
REP = ("ra", "rb", "rc")
ARC = ("rb", "rc")
QUAD = "rc"
MASKED = -1e30
NONE_VISIBLE = -1e29
F32, BF16 = jnp.float32, jnp.bfloat16


def exchanged(pieces, axes):
    return lax.all_to_all(pieces, axes, split_axis=0, concat_axis=0, tiled=True)


def permuted(array, axes, count, target):
    return lax.ppermute(array, axes, [(i, target(i)) for i in range(count)])


def dot_rows(a, b):
    return lax.dot_general(a, b, (((1,), (1,)), ((), ())), preferred_element_type=F32)


def stacked(pieces, axis=0):
    return jnp.concatenate(pieces, axis=axis)


def attend_kernel(first, len_ref, q_ref, nk_ref, nv_ref, k_ref, v_ref, *refs):
    *earlier_ref, out_ref, stats_ref = refs
    b = first + pl.program_id(0)
    rows_b = out_ref.shape[1] - 1
    _, steps, width = q_ref.shape
    head_dim = k_ref.shape[2]
    kv_heads = nk_ref.shape[1] // steps
    heads = width // head_dim
    rows = heads * steps
    columns = k_ref.shape[1]
    block_len = columns // kv_heads
    to_log2 = math.log2(math.e) / math.sqrt(head_dim)
    tp = lax.axis_index("tp")

    def own_head(count):
        row = lax.broadcasted_iota(jnp.int32, (rows, count), 0)
        column = lax.broadcasted_iota(jnp.int32, (rows, count), 1)
        same = (column % kv_heads) == (row // (rows // kv_heads))
        return row, column // kv_heads, same

    def masked(key_ref, visible):
        return jnp.where(visible, dot_rows(q, key_ref[0]) * to_log2, MASKED)

    _, position, same = own_head(columns)
    visible = same & (position < len_ref[b] - tp * block_len)
    row, fresh_at, same = own_head(nk_ref.shape[1])
    fresh_visible = same & (fresh_at <= row % steps) & (tp == 0)
    wide = q_ref[0].astype(F32)
    q = stacked([wide[:, h * head_dim : (h + 1) * head_dim] for h in range(heads)]).astype(BF16)
    scores, fresh = masked(k_ref, visible), masked(nk_ref, fresh_visible)
    top = jnp.maximum(scores.max(1, keepdims=True), fresh.max(1, keepdims=True))
    shift = jnp.maximum(top, NONE_VISIBLE).astype(BF16).astype(F32)
    weights, fresh_weights = jnp.exp2(scores - shift), jnp.exp2(fresh - shift)
    total = weights.sum(1, keepdims=True) + fresh_weights.sum(1, keepdims=True)
    numerator = jnp.dot(weights.astype(BF16), v_ref[0], preferred_element_type=F32)
    numerator += jnp.dot(fresh_weights.astype(BF16), nv_ref[0], preferred_element_type=F32)
    out_ref[:, b] = numerator.astype(BF16).reshape(-1, 8, head_dim)
    high = total.astype(BF16).astype(F32)
    lane = lax.broadcasted_iota(jnp.int32, (rows, head_dim), 1)
    if earlier_ref:
        earlier = earlier_ref[0][:, first].astype(F32).reshape(rows, head_dim)

        @pl.when(b == first)
        def _():
            out_ref[:, :first] = earlier_ref[0][:, :first]

    else:
        earlier = jnp.zeros((rows, head_dim), F32)
    stats = jnp.where(b == first, earlier, stats_ref[...])
    stats = jnp.where(lane == 3 * b, shift, stats)
    stats = jnp.where(lane == 3 * b + 1, high, stats)
    stats = jnp.where(lane == 3 * b + 2, total - high, stats)
    stats_ref[...] = stats
    out_ref[:, rows_b] = stats.astype(BF16).reshape(-1, 8, head_dim)


def attend(queries, new_keys, new_values, keys, values, lengths, first, last, *earlier):
    arrays = (queries, new_keys, new_values, keys, values)
    head_dim = keys.shape[2]
    pieces = queries.shape[2] * queries.shape[1] // head_dim // 8
    outs = jax.ShapeDtypeStruct((pieces, last + 1, 8, head_dim), BF16)
    whole = pl.BlockSpec(outs.shape, lambda b: (0, 0, 0, 0))
    before = [pl.BlockSpec(a.shape, lambda b: (0, 0, 0, 0)) for a in earlier]
    return pl.pallas_call(
        functools.partial(attend_kernel, first),
        grid=(last - first,),
        out_shape=outs,
        in_specs=[
            pl.BlockSpec(memory_space=pltpu.SMEM),
            *(pl.BlockSpec((1, *a.shape[1:]), lambda b: (first + b, 0, 0)) for a in arrays),
            *before,
        ],
        out_specs=whole,
        scratch_shapes=[pltpu.VMEM((pieces * 8, head_dim), F32)],
        compiler_params=pltpu.CompilerParams(vmem_limit_bytes=60 * 1024 * 1024),
        cost_estimate=pl.CostEstimate(
            flops=150_000_000, bytes_accessed=keys.size * 2, transcendentals=300_000
        ),
    )(lengths, *arrays, *earlier)


def combine_kernel(parts_ref, out_ref):
    rows_b = parts_ref.shape[1] - 1
    half = parts_ref.shape[2] // 2
    stats = parts_ref[:, rows_b].astype(F32)
    first, second = [], []
    for b in range(rows_b):
        shift, high, low = (stats[:, :, 3 * b + i : 3 * b + i + 1] for i in range(3))
        scale = jnp.exp2(shift - shift.max(0, keepdims=True))
        total = jnp.sum(scale * (high + low), axis=0)
        numerator = jnp.sum(scale * parts_ref[:, b].astype(F32), axis=0)
        attended = numerator / total
        first.append(attended[:half])
        second.append(attended[half:])
    attended = stacked([stacked(first), stacked(second)], 1).astype(BF16)
    for i in range(out_ref.shape[0]):
        out_ref[i] = attended


def side_by_side_kernel(blocks_ref, out_ref):
    for j in range(blocks_ref.shape[0]):
        out_ref[:, j * 128 : (j + 1) * 128] = blocks_ref[j]


def project_kernel(x_ref, w_ref, out_ref):
    x = x_ref[...].reshape(-1, x_ref.shape[2])
    projected = jnp.dot(x, w_ref[...], preferred_element_type=F32)
    out_ref[...] = projected.astype(BF16).reshape(out_ref.shape)


def sum_kernel(parts_ref, out_ref):
    out_ref[...] = jnp.sum(parts_ref[...].astype(F32), axis=0).astype(BF16)


def hidden_kernel(summed_ref, stream_ref, hidden_ref, squares_ref):
    stream = stacked([stream_ref[b].astype(F32) for b in range(stream_ref.shape[0])])
    hidden = stream + summed_ref[...].astype(F32)
    hidden_ref[...] = hidden
    squares = hidden * hidden
    squares = sum(squares[:, j : j + 128] for j in range(0, squares.shape[1], 128))
    for i in range(squares_ref.shape[0]):
        squares_ref[i] = squares


def norm_kernel(squares_ref, hidden_ref, gain_ref, stream_ref, normed_ref):
    squares = jnp.sum(jnp.sum(squares_ref[...], axis=0), axis=1, keepdims=True)
    hidden = hidden_ref[...]
    normed = hidden * lax.rsqrt(squares / D + 1e-06) * gain_ref[...].astype(F32)
    rows_b, steps, _ = stream_ref.shape
    for b in range(rows_b):
        stream_ref[b] = hidden[b * steps : (b + 1) * steps].astype(BF16)
        normed_ref[b] = normed[b * steps : (b + 1) * steps].astype(BF16)


def call(kernel, outs, *args, flops=0):
    single = not isinstance(outs, list)
    size = sum(a.size * a.dtype.itemsize for a in args)
    vmem = pl.BlockSpec(memory_space=pltpu.VMEM)
    return pl.pallas_call(
        kernel,
        out_shape=outs,
        in_specs=[vmem] * len(args),
        out_specs=vmem if single else [vmem] * len(outs),
        compiler_params=pltpu.CompilerParams(vmem_limit_bytes=32 * 1024 * 1024),
        cost_estimate=pl.CostEstimate(flops=flops, bytes_accessed=size, transcendentals=0),
    )(*args)


def on_device(
    stream_in, queries, new_keys, new_values, key_cache, value_cache, lengths, out_weight, norm_gain
):
    rows_b, steps, width = queries.shape
    kv_heads, head_dim = key_cache.shape[2:]
    n_tp, n_arc = lax.axis_size("tp"), lax.axis_size(ARC)
    n_quad = lax.axis_size(QUAD)
    n_rep = n_arc * lax.axis_size("ra")
    rows = rows_b * steps
    columns = stream_in.shape[2]
    share = width // n_tp

    with jax.named_scope("weights"):
        quad = exchanged(jnp.broadcast_to(out_weight, (n_quad, *out_weight.shape)), QUAD)

    with jax.named_scope("attention"):
        flat = lambda a: a.reshape(rows_b, -1, head_dim)
        cached = (flat(new_keys), flat(new_values), flat(key_cache), flat(value_cache))
        half = rows_b // 2
        parts = attend(queries, *cached, lengths, 0, half)
        parts, quad = lax.optimization_barrier((parts, quad))
        parts = attend(queries, *cached, lengths, half, rows_b, parts)
        weight = permuted(quad, REP, n_rep, lambda r: (r % n_quad) * n_arc + r // n_quad)
        weight = call(
            side_by_side_kernel, jax.ShapeDtypeStruct((share, columns), BF16), weight, flops=20_000_000_000
        )
        parts = exchanged(parts, "tp")
        attended = call(combine_kernel, jax.ShapeDtypeStruct((n_arc, rows, share), BF16), parts)
        attended = exchanged(attended, ARC)

    with jax.named_scope("projection"):
        projected = call(
            project_kernel, jax.ShapeDtypeStruct((n_arc, rows, columns), BF16), attended, weight,
            flops=2 * n_arc * rows * share * columns,
        )
        partials = exchanged(projected, "tp")
        summed = call(sum_kernel, jax.ShapeDtypeStruct((rows, columns), BF16), partials)

        def home(i):
            r, p = i // n_tp, i % n_tp
            return (r // n_arc * n_arc + p) * n_tp + r % n_arc

        summed = permuted(summed, (*REP, "tp"), n_rep * n_tp, home)

    with jax.named_scope("norm"):
        hidden, squares = call(
            hidden_kernel,
            [
                jax.ShapeDtypeStruct((rows, columns), F32),
                jax.ShapeDtypeStruct((n_tp, rows, 128), F32),
            ],
            summed, stream_in,
        )
        squares = exchanged(squares, "tp")
        out = jax.ShapeDtypeStruct(stream_in.shape, BF16)
        return tuple(call(norm_kernel, [out, out], squares, hidden, norm_gain.reshape(1, -1)))


def solution(mesh):
    finer = Mesh(mesh.devices.reshape(4, 4, 4, mesh.shape["tp"]), (*REP, "tp"))
    in_specs = (
        P(REP, None, "tp"),
        P(REP, None, None),
        P(REP, None, None, None),
        P(REP, None, None, None),
        P(REP, "tp", None, None),
        P(REP, "tp", None, None),
        P(REP),
        P("tp", REP),
        P("tp"),
    )
    out_specs = (P(REP, None, "tp"), P(REP, None, "tp"))
    return jax.shard_map(
        on_device, mesh=finer, in_specs=in_specs, out_specs=out_specs, check_vma=False
    )
```

```python
import functools
import math

import jax
import jax.numpy as jnp
from jax import lax
from jax.experimental import pallas as pl
from jax.experimental.pallas import tpu as pltpu
from jax.sharding import Mesh
from jax.sharding import PartitionSpec as P

D = 8192
REP = ("ra", "rb", "rc")
ARC = ("rb", "rc")
QUAD = "rc"
MASKED = -1e30
NONE_VISIBLE = -1e29
F32, BF16 = jnp.float32, jnp.bfloat16


def exchanged(pieces, axes):
    return lax.all_to_all(pieces, axes, split_axis=0, concat_axis=0, tiled=True)


def permuted(array, axes, count, target):
    return lax.ppermute(array, axes, [(i, target(i)) for i in range(count)])


def dot_rows(a, b):
    return lax.dot_general(a, b, (((1,), (1,)), ((), ())), preferred_element_type=F32)


def stacked(pieces, axis=0):
    return jnp.concatenate(pieces, axis=axis)


def tiled(wide):
    rows, columns = wide.shape
    cut = [wide[:, j : j + 128].reshape(rows, 1, 128) for j in range(0, columns, 128)]
    return stacked([*cut, jnp.zeros((rows, 8 - len(cut), 128), wide.dtype)], 1)


def attend_kernel(first, last, len_ref, q_ref, nk_ref, nv_ref, k_ref, v_ref, *refs):
    *earlier_ref, out_ref, stats_ref = refs
    b = first + pl.program_id(0)
    _, steps, width = q_ref.shape
    head_dim = k_ref.shape[2]
    kv_heads = nk_ref.shape[1] // steps
    heads = width // head_dim
    rows = heads * steps
    columns = k_ref.shape[1]
    block_len = columns // kv_heads
    to_log2 = math.log2(math.e) / math.sqrt(head_dim)
    tp = lax.axis_index("tp")

    def own_head(count):
        row = lax.broadcasted_iota(jnp.int32, (rows, count), 0)
        column = lax.broadcasted_iota(jnp.int32, (rows, count), 1)
        same = (column % kv_heads) == (row // (rows // kv_heads))
        return row, column // kv_heads, same

    def masked(key_ref, visible):
        return jnp.where(visible, dot_rows(q, key_ref[0]) * to_log2, MASKED)

    _, position, same = own_head(columns)
    visible = same & (position < len_ref[b] - tp * block_len)
    row, fresh_at, same = own_head(nk_ref.shape[1])
    fresh_visible = same & (fresh_at <= row % steps) & (tp == 0)
    wide = q_ref[0].astype(F32)
    q = stacked([wide[:, h * head_dim : (h + 1) * head_dim] for h in range(heads)]).astype(BF16)
    scores, fresh = masked(k_ref, visible), masked(nk_ref, fresh_visible)
    top = jnp.maximum(scores.max(1, keepdims=True), fresh.max(1, keepdims=True))
    shift = jnp.maximum(top, NONE_VISIBLE).astype(BF16).astype(F32)
    weights, fresh_weights = jnp.exp2(scores - shift), jnp.exp2(fresh - shift)
    total = weights.sum(1, keepdims=True) + fresh_weights.sum(1, keepdims=True)
    numerator = jnp.dot(weights.astype(BF16), v_ref[0], preferred_element_type=F32)
    numerator += jnp.dot(fresh_weights.astype(BF16), nv_ref[0], preferred_element_type=F32)
    out_ref[:, b] = numerator.astype(BF16).reshape(-1, 8, head_dim)
    high = total.astype(BF16).astype(F32)
    lane = lax.broadcasted_iota(jnp.int32, (rows, head_dim), 1)
    if earlier_ref:
        earlier = earlier_ref[0][:, first].astype(F32).reshape(rows, head_dim)

        @pl.when(b == first)
        def _():
            out_ref[:, :first] = earlier_ref[0][:, :first]
            stream = stacked([earlier_ref[1][r].astype(F32) for r in range(last)])
            out_ref[:, last + 1] = tiled(stream).astype(BF16)

    else:
        earlier = jnp.zeros((rows, head_dim), F32)
    stats = jnp.where(b == first, earlier, stats_ref[...])
    stats = jnp.where(lane == 3 * b, shift, stats)
    stats = jnp.where(lane == 3 * b + 1, high, stats)
    stats = jnp.where(lane == 3 * b + 2, total - high, stats)
    stats_ref[...] = stats
    out_ref[:, last] = stats.astype(BF16).reshape(-1, 8, head_dim)


def zeros(count, _):
    return (0,) * count


def attend(queries, new_keys, new_values, keys, values, lengths, first, last, *earlier):
    arrays = (queries, new_keys, new_values, keys, values)
    head_dim = keys.shape[2]
    pieces = queries.shape[2] * queries.shape[1] // head_dim // 8
    outs = jax.ShapeDtypeStruct((pieces, last + 1 + (len(earlier) > 1), 8, head_dim), BF16)
    whole = pl.BlockSpec(outs.shape, lambda b: (0, 0, 0, 0))
    before = [pl.BlockSpec(a.shape, functools.partial(zeros, a.ndim)) for a in earlier]
    return pl.pallas_call(
        functools.partial(attend_kernel, first, last),
        grid=(last - first,),
        out_shape=outs,
        in_specs=[
            pl.BlockSpec(memory_space=pltpu.SMEM),
            *(pl.BlockSpec((1, *a.shape[1:]), lambda b: (first + b, 0, 0)) for a in arrays),
            *before,
        ],
        out_specs=whole,
        scratch_shapes=[pltpu.VMEM((pieces * 8, head_dim), F32)],
        compiler_params=pltpu.CompilerParams(vmem_limit_bytes=60 * 1024 * 1024),
        cost_estimate=pl.CostEstimate(
            flops=150_000_000, bytes_accessed=keys.size * 2, transcendentals=300_000
        ),
    )(lengths, *arrays, *earlier)


def combine_kernel(parts_ref, out_ref, stream_ref):
    rows_b = parts_ref.shape[1] - 2
    half = parts_ref.shape[2] // 2
    stats = parts_ref[:, rows_b].astype(F32)
    first, second = [], []
    for b in range(rows_b):
        shift, high, low = (stats[:, :, 3 * b + i : 3 * b + i + 1] for i in range(3))
        scale = jnp.exp2(shift - shift.max(0, keepdims=True))
        total = jnp.sum(scale * (high + low), axis=0)
        numerator = jnp.sum(scale * parts_ref[:, b].astype(F32), axis=0)
        attended = numerator / total
        first.append(attended[:half])
        second.append(attended[half:])
    attended = stacked([stacked(first), stacked(second)], 1).astype(BF16)
    for i in range(out_ref.shape[0]):
        out_ref[i] = attended
    stream_ref[...] = parts_ref[:, rows_b + 1].astype(F32)


def side_by_side_kernel(blocks_ref, out_ref):
    for j in range(blocks_ref.shape[0]):
        out_ref[:, j * 128 : (j + 1) * 128] = blocks_ref[j]


def project_kernel(x_ref, w_ref, out_ref):
    x = jnp.swapaxes(x_ref[...].astype(F32), 0, 1).astype(BF16)
    projected = jnp.dot(x.reshape(-1, x.shape[2]), w_ref[...], preferred_element_type=F32)
    out_ref[...] = projected.astype(BF16).reshape(out_ref.shape)


def sum_kernel(parts_ref, out_ref):
    out_ref[...] = tiled(jnp.sum(parts_ref[...].astype(F32), axis=0))


def hidden_kernel(summed_ref, stream_ref, out_ref):
    hidden = summed_ref[...] + stream_ref[...]
    squares = jnp.sum(hidden * hidden, axis=0)
    squares = jnp.sum(jnp.sum(squares, axis=0, keepdims=True), axis=1, keepdims=True)
    inverse = lax.rsqrt(squares / D + 1e-06).reshape(1, 1, 1)
    line = lax.broadcasted_iota(jnp.int32, hidden.shape, 1)
    out_ref[...] = jnp.where(line == hidden.shape[1] - 1, inverse, hidden)


def norm_kernel(tiles_ref, gain_ref, stream_ref, normed_ref):
    rows_b, steps, columns = stream_ref.shape
    hidden = stacked([tiles_ref[:, j, :] for j in range(columns // 128)], 1)
    inverse = tiles_ref[:, tiles_ref.shape[1] - 1, :][:, :1]
    normed = hidden * inverse * gain_ref[...].astype(F32)
    for b in range(rows_b):
        stream_ref[b] = hidden[b * steps : (b + 1) * steps].astype(BF16)
        normed_ref[b] = normed[b * steps : (b + 1) * steps].astype(BF16)


def call(kernel, outs, *args, flops=0):
    single = not isinstance(outs, list)
    size = sum(a.size * a.dtype.itemsize for a in args)
    vmem = pl.BlockSpec(memory_space=pltpu.VMEM)
    return pl.pallas_call(
        kernel,
        out_shape=outs,
        in_specs=[vmem] * len(args),
        out_specs=vmem if single else [vmem] * len(outs),
        compiler_params=pltpu.CompilerParams(vmem_limit_bytes=32 * 1024 * 1024),
        cost_estimate=pl.CostEstimate(flops=flops, bytes_accessed=size, transcendentals=0),
    )(*args)


def on_device(
    stream_in, queries, new_keys, new_values, key_cache, value_cache, lengths, out_weight, norm_gain
):
    rows_b, steps, width = queries.shape
    kv_heads, head_dim = key_cache.shape[2:]
    n_tp, n_arc = lax.axis_size("tp"), lax.axis_size(ARC)
    n_quad = lax.axis_size(QUAD)
    n_rep = n_arc * lax.axis_size("ra")
    rows = rows_b * steps
    columns = stream_in.shape[2]
    share = width // n_tp

    with jax.named_scope("weights"):
        quad = exchanged(jnp.broadcast_to(out_weight, (n_quad, *out_weight.shape)), QUAD)

    with jax.named_scope("attention"):
        flat = lambda a: a.reshape(rows_b, -1, head_dim)
        cached = (flat(new_keys), flat(new_values), flat(key_cache), flat(value_cache))
        half = rows_b // 2
        parts = attend(queries, *cached, lengths, 0, half)
        parts, quad = lax.optimization_barrier((parts, quad))
        parts = attend(queries, *cached, lengths, half, rows_b, parts, stream_in)
        weight = permuted(quad, REP, n_rep, lambda r: (r % n_quad) * n_arc + r // n_quad)
        weight = call(
            side_by_side_kernel, jax.ShapeDtypeStruct((share, columns), BF16), weight, flops=20_000_000_000
        )
        parts = exchanged(parts, "tp")
        tiles = jax.ShapeDtypeStruct((n_tp, 8, 128), F32)
        attended, stream = call(
            combine_kernel, [jax.ShapeDtypeStruct((n_arc, rows, share), BF16), tiles], parts
        )
        attended = exchanged(attended, ARC)

    with jax.named_scope("projection"):
        projected = call(
            project_kernel, jax.ShapeDtypeStruct((rows, n_arc, columns), BF16), attended, weight,
            flops=2 * n_arc * rows * share * columns,
        )
        partials = exchanged(projected, "tp")
        summed = exchanged(call(sum_kernel, tiles, partials), ARC)

    with jax.named_scope("norm"):
        hidden = exchanged(call(hidden_kernel, tiles, summed, stream), "tp")
        out = jax.ShapeDtypeStruct(stream_in.shape, BF16)
        return tuple(call(norm_kernel, [out, out], hidden, norm_gain.reshape(1, -1)))


def solution(mesh):
    finer = Mesh(mesh.devices.reshape(4, 4, 4, mesh.shape["tp"]), (*REP, "tp"))
    in_specs = (
        P(REP, None, "tp"),
        P(REP, None, None),
        P(REP, None, None, None),
        P(REP, None, None, None),
        P(REP, "tp", None, None),
        P(REP, "tp", None, None),
        P(REP),
        P("tp", REP),
        P("tp"),
    )
    out_specs = (P(REP, None, "tp"), P(REP, None, "tp"))
    return jax.shard_map(
        on_device, mesh=finer, in_specs=in_specs, out_specs=out_specs, check_vma=False
    )
```

```python
import math

import jax
import jax.numpy as jnp
from jax import lax
from jax.experimental import pallas as pl
from jax.experimental.pallas import tpu as pltpu
from jax.sharding import Mesh
from jax.sharding import PartitionSpec as P

D = 8192
REP = ("ra", "rb", "rc")
ARC = ("rb", "rc")
QUAD = "rc"
MASKED = -1e30
NONE_VISIBLE = -1e29
F32, BF16 = jnp.float32, jnp.bfloat16


def exchanged(pieces, axes):
    return lax.all_to_all(pieces, axes, split_axis=0, concat_axis=0, tiled=True)


def permuted(array, axes, count, target):
    return lax.ppermute(array, axes, [(i, target(i)) for i in range(count)])


def dot_rows(a, b):
    return lax.dot_general(a, b, (((1,), (1,)), ((), ())), preferred_element_type=F32)


def stacked(pieces, axis=0):
    return jnp.concatenate(pieces, axis=axis)


def attend_kernel(len_ref, q_ref, nk_ref, nv_ref, k_ref, v_ref, out_ref, stats_ref):
    b = pl.program_id(0)
    rows_b = pl.num_programs(0)
    _, steps, width = q_ref.shape
    head_dim = k_ref.shape[2]
    kv_heads = nk_ref.shape[1] // steps
    heads = width // head_dim
    rows = heads * steps
    columns = k_ref.shape[1]
    block_len = columns // kv_heads
    to_log2 = math.log2(math.e) / math.sqrt(head_dim)
    tp = lax.axis_index("tp")

    def own_head(count):
        row = lax.broadcasted_iota(jnp.int32, (rows, count), 0)
        column = lax.broadcasted_iota(jnp.int32, (rows, count), 1)
        same = (column % kv_heads) == (row // (rows // kv_heads))
        return row, column // kv_heads, same

    def masked(key_ref, visible):
        return jnp.where(visible, dot_rows(q, key_ref[0]) * to_log2, MASKED)

    _, position, same = own_head(columns)
    visible = same & (position < len_ref[b] - tp * block_len)
    row, fresh_at, same = own_head(nk_ref.shape[1])
    fresh_visible = same & (fresh_at <= row % steps) & (tp == 0)
    wide = q_ref[0].astype(F32)
    q = stacked([wide[:, h * head_dim : (h + 1) * head_dim] for h in range(heads)]).astype(BF16)
    scores, fresh = masked(k_ref, visible), masked(nk_ref, fresh_visible)
    top = jnp.maximum(scores.max(1, keepdims=True), fresh.max(1, keepdims=True))
    shift = jnp.maximum(top, NONE_VISIBLE).astype(BF16).astype(F32)
    weights, fresh_weights = jnp.exp2(scores - shift), jnp.exp2(fresh - shift)
    total = weights.sum(1, keepdims=True) + fresh_weights.sum(1, keepdims=True)
    numerator = jnp.dot(weights.astype(BF16), v_ref[0], preferred_element_type=F32)
    numerator += jnp.dot(fresh_weights.astype(BF16), nv_ref[0], preferred_element_type=F32)
    out_ref[:, b] = numerator.astype(BF16).reshape(-1, 8, head_dim)
    high = total.astype(BF16).astype(F32)
    lane = lax.broadcasted_iota(jnp.int32, (rows, head_dim), 1)
    stats = jnp.where(b == 0, jnp.zeros((rows, head_dim), F32), stats_ref[...])
    stats = jnp.where(lane == 3 * b, shift, stats)
    stats = jnp.where(lane == 3 * b + 1, high, stats)
    stats = jnp.where(lane == 3 * b + 2, total - high, stats)
    stats_ref[...] = stats
    out_ref[:, rows_b] = stats.astype(BF16).reshape(-1, 8, head_dim)


def attend(queries, new_keys, new_values, keys, values, lengths, outs):
    def of_row(a):
        return pl.BlockSpec((1, *a.shape[1:]), lambda b: (b, 0, 0))

    return pl.pallas_call(
        attend_kernel,
        grid=(queries.shape[0],),
        out_shape=outs,
        in_specs=[
            pl.BlockSpec(memory_space=pltpu.SMEM),
            *(of_row(a) for a in (queries, new_keys, new_values, keys, values)),
        ],
        out_specs=pl.BlockSpec(outs.shape, lambda b: (0, 0, 0, 0)),
        scratch_shapes=[pltpu.VMEM((outs.shape[0] * outs.shape[2], outs.shape[3]), F32)],
        compiler_params=pltpu.CompilerParams(vmem_limit_bytes=60 * 1024 * 1024),
        cost_estimate=pl.CostEstimate(
            flops=300_000_000, bytes_accessed=2 * keys.size * 2, transcendentals=600_000
        ),
    )(lengths, queries, new_keys, new_values, keys, values)


def combine_kernel(parts_ref, out_ref):
    rows_b = parts_ref.shape[1] - 1
    half = parts_ref.shape[2] // 2
    stats = parts_ref[:, rows_b].astype(F32)
    first, second = [], []
    for b in range(rows_b):
        shift, high, low = (stats[:, :, 3 * b + i : 3 * b + i + 1] for i in range(3))
        scale = jnp.exp2(shift - shift.max(0, keepdims=True))
        total = jnp.sum(scale * (high + low), axis=0)
        numerator = jnp.sum(scale * parts_ref[:, b].astype(F32), axis=0)
        attended = numerator / total
        first.append(attended[:half])
        second.append(attended[half:])
    attended = stacked([stacked(first), stacked(second)], 1).astype(BF16)
    for i in range(out_ref.shape[0]):
        out_ref[i] = attended


def side_by_side_kernel(blocks_ref, out_ref):
    for j in range(blocks_ref.shape[0]):
        out_ref[:, j * 128 : (j + 1) * 128] = blocks_ref[j]


def project_kernel(x_ref, w_ref, out_ref):
    x = x_ref[...].reshape(-1, x_ref.shape[2])
    projected = jnp.dot(x, w_ref[...], preferred_element_type=F32)
    out_ref[...] = projected.astype(BF16).reshape(out_ref.shape)


def sum_kernel(parts_ref, out_ref):
    out_ref[...] = jnp.sum(parts_ref[...].astype(F32), axis=0).astype(BF16)


def hidden_kernel(summed_ref, stream_ref, hidden_ref, squares_ref):
    stream = stacked([stream_ref[b].astype(F32) for b in range(stream_ref.shape[0])])
    hidden = stream + summed_ref[...].astype(F32)
    hidden_ref[...] = hidden
    squares = hidden * hidden
    squares = sum(squares[:, j : j + 128] for j in range(0, squares.shape[1], 128))
    for i in range(squares_ref.shape[0]):
        squares_ref[i] = squares


def norm_kernel(squares_ref, hidden_ref, gain_ref, stream_ref, normed_ref):
    squares = jnp.sum(jnp.sum(squares_ref[...], axis=0), axis=1, keepdims=True)
    hidden = hidden_ref[...]
    normed = hidden * lax.rsqrt(squares / D + 1e-06) * gain_ref[...].astype(F32)
    rows_b, steps, _ = stream_ref.shape
    for b in range(rows_b):
        stream_ref[b] = hidden[b * steps : (b + 1) * steps].astype(BF16)
        normed_ref[b] = normed[b * steps : (b + 1) * steps].astype(BF16)


def call(kernel, outs, *args, flops=0):
    single = not isinstance(outs, list)
    size = sum(a.size * a.dtype.itemsize for a in args)
    vmem = pl.BlockSpec(memory_space=pltpu.VMEM)
    return pl.pallas_call(
        kernel,
        out_shape=outs,
        in_specs=[vmem] * len(args),
        out_specs=vmem if single else [vmem] * len(outs),
        compiler_params=pltpu.CompilerParams(vmem_limit_bytes=32 * 1024 * 1024),
        cost_estimate=pl.CostEstimate(flops=flops, bytes_accessed=size, transcendentals=0),
    )(*args)


def on_device(
    stream_in, queries, new_keys, new_values, key_cache, value_cache, lengths, out_weight, norm_gain
):
    rows_b, steps, width = queries.shape
    kv_heads, head_dim = key_cache.shape[2:]
    n_tp, n_arc = lax.axis_size("tp"), lax.axis_size(ARC)
    n_quad = lax.axis_size(QUAD)
    n_rep = n_arc * lax.axis_size("ra")
    rows = rows_b * steps
    columns = stream_in.shape[2]
    share = width // n_tp

    def place_of(arc, quad):
        return (quad - arc * n_quad + 6) % n_arc

    def columns_of(arc, place):
        return (place - 6 + arc * n_quad) % n_arc

    def weight_home(r):
        quad, member = r // n_quad, r % n_quad
        arc = (quad // n_quad - member) % n_quad
        return arc * n_arc + place_of(arc, quad)

    with jax.named_scope("weights"):
        quad = exchanged(jnp.broadcast_to(out_weight, (n_quad, *out_weight.shape)), QUAD)

    with jax.named_scope("attention"):
        flat = lambda a: a.reshape(rows_b, -1, head_dim)
        parts = attend(
            queries, flat(new_keys), flat(new_values), flat(key_cache), flat(value_cache), lengths,
            jax.ShapeDtypeStruct((n_tp, rows_b + 1, 8, head_dim), BF16),
        )
        parts, quad = lax.optimization_barrier((parts, quad))
        weight = permuted(quad, REP, n_rep, weight_home)
        weight = call(
            side_by_side_kernel, jax.ShapeDtypeStruct((share, columns), BF16), weight, flops=20_000_000_000
        )
        parts = exchanged(parts, "tp")
        attended = call(combine_kernel, jax.ShapeDtypeStruct((n_arc, rows, share), BF16), parts)
        attended = exchanged(attended, ARC)

    with jax.named_scope("projection"):
        projected = call(
            project_kernel, jax.ShapeDtypeStruct((n_arc, rows, columns), BF16), attended, weight,
            flops=2 * n_arc * rows * share * columns,
        )
        partials = exchanged(projected, "tp")
        summed = call(sum_kernel, jax.ShapeDtypeStruct((rows, columns), BF16), partials)

        def home(i):
            arc, place, p = i // (n_arc * n_tp), i // n_tp % n_arc, i % n_tp
            return (arc * n_arc + p) * n_tp + columns_of(arc, place)

        summed = permuted(summed, (*REP, "tp"), n_rep * n_tp, home)

    with jax.named_scope("norm"):
        hidden, squares = call(
            hidden_kernel,
            [
                jax.ShapeDtypeStruct((rows, columns), F32),
                jax.ShapeDtypeStruct((n_tp, rows, 128), F32),
            ],
            summed, stream_in,
        )
        squares = exchanged(squares, "tp")
        out = jax.ShapeDtypeStruct(stream_in.shape, BF16)
        return tuple(call(norm_kernel, [out, out], squares, hidden, norm_gain.reshape(1, -1)))


def solution(mesh):
    finer = Mesh(mesh.devices.reshape(4, 4, 4, mesh.shape["tp"]), (*REP, "tp"))
    in_specs = (
        P(REP, None, "tp"),
        P(REP, None, None),
        P(REP, None, None, None),
        P(REP, None, None, None),
        P(REP, "tp", None, None),
        P(REP, "tp", None, None),
        P(REP),
        P("tp", REP),
        P("tp"),
    )
    out_specs = (P(REP, None, "tp"), P(REP, None, "tp"))
    return jax.shard_map(
        on_device, mesh=finer, in_specs=in_specs, out_specs=out_specs, check_vma=False
    )
```

```python
import math

import jax
import jax.numpy as jnp
from jax import lax
from jax.experimental import pallas as pl
from jax.experimental.pallas import tpu as pltpu
from jax.sharding import Mesh
from jax.sharding import PartitionSpec as P

D = 8192
REP = ("ra", "rb", "rc")
ARC = ("rb", "rc")
QUAD = "rc"
MASKED = -1e30
NONE_VISIBLE = -1e29
F32, BF16 = jnp.float32, jnp.bfloat16


def exchanged(pieces, axes):
    return lax.all_to_all(pieces, axes, split_axis=0, concat_axis=0, tiled=True)


def permuted(array, axes, count, target):
    return lax.ppermute(array, axes, [(i, target(i)) for i in range(count)])


def dot_rows(a, b):
    return lax.dot_general(a, b, (((1,), (1,)), ((), ())), preferred_element_type=F32)


def stacked(pieces, axis=0):
    return jnp.concatenate(pieces, axis=axis)


def attend_kernel(len_ref, q_ref, nk_ref, nv_ref, k_ref, v_ref, out_ref, stats_ref):
    b = pl.program_id(0)
    rows_b = pl.num_programs(0)
    _, steps, width = q_ref.shape
    head_dim = k_ref.shape[2]
    kv_heads = nk_ref.shape[1] // steps
    heads = width // head_dim
    rows = heads * steps
    columns = k_ref.shape[1]
    block_len = columns // kv_heads
    to_log2 = math.log2(math.e) / math.sqrt(head_dim)
    tp = lax.axis_index("tp")

    def own_head(count):
        row = lax.broadcasted_iota(jnp.int32, (rows, count), 0)
        column = lax.broadcasted_iota(jnp.int32, (rows, count), 1)
        same = (column % kv_heads) == (row // (rows // kv_heads))
        return row, column // kv_heads, same

    def masked(key_ref, visible):
        return jnp.where(visible, dot_rows(q, key_ref[0]) * to_log2, MASKED)

    _, position, same = own_head(columns)
    visible = same & (position < len_ref[b] - tp * block_len)
    row, fresh_at, same = own_head(nk_ref.shape[1])
    fresh_visible = same & (fresh_at <= row % steps) & (tp == 0)
    wide = q_ref[0].astype(F32)
    q = stacked([wide[:, h * head_dim : (h + 1) * head_dim] for h in range(heads)]).astype(BF16)
    scores, fresh = masked(k_ref, visible), masked(nk_ref, fresh_visible)
    top = jnp.maximum(scores.max(1, keepdims=True), fresh.max(1, keepdims=True))
    shift = jnp.maximum(top, NONE_VISIBLE).astype(BF16).astype(F32)
    weights, fresh_weights = jnp.exp2(scores - shift), jnp.exp2(fresh - shift)
    total = weights.sum(1, keepdims=True) + fresh_weights.sum(1, keepdims=True)
    numerator = jnp.dot(weights.astype(BF16), v_ref[0], preferred_element_type=F32)
    numerator += jnp.dot(fresh_weights.astype(BF16), nv_ref[0], preferred_element_type=F32)
    out_ref[:, b] = numerator.astype(BF16).reshape(-1, 8, head_dim)
    high = total.astype(BF16).astype(F32)
    lane = lax.broadcasted_iota(jnp.int32, (rows, head_dim), 1)
    stats = jnp.where(b == 0, jnp.zeros((rows, head_dim), F32), stats_ref[...])
    stats = jnp.where(lane == 3 * b, shift, stats)
    stats = jnp.where(lane == 3 * b + 1, high, stats)
    stats = jnp.where(lane == 3 * b + 2, total - high, stats)
    stats_ref[...] = stats
    out_ref[:, rows_b] = stats.astype(BF16).reshape(-1, 8, head_dim)


def attend(queries, new_keys, new_values, keys, values, lengths, outs):
    def of_row(a):
        return pl.BlockSpec((1, *a.shape[1:]), lambda b: (b, 0, 0))

    return pl.pallas_call(
        attend_kernel,
        grid=(queries.shape[0],),
        out_shape=outs,
        in_specs=[
            pl.BlockSpec(memory_space=pltpu.SMEM),
            *(of_row(a) for a in (queries, new_keys, new_values, keys, values)),
        ],
        out_specs=pl.BlockSpec(outs.shape, lambda b: (0, 0, 0, 0)),
        scratch_shapes=[pltpu.VMEM((outs.shape[0] * outs.shape[2], outs.shape[3]), F32)],
        compiler_params=pltpu.CompilerParams(vmem_limit_bytes=60 * 1024 * 1024),
        cost_estimate=pl.CostEstimate(
            flops=300_000_000, bytes_accessed=2 * keys.size * 2, transcendentals=600_000
        ),
    )(lengths, queries, new_keys, new_values, keys, values)


def combine_kernel(parts_ref, out_ref):
    rows_b = parts_ref.shape[1] - 1
    half = parts_ref.shape[2] // 2
    stats = parts_ref[:, rows_b].astype(F32)
    first, second = [], []
    for b in range(rows_b):
        shift, high, low = (stats[:, :, 3 * b + i : 3 * b + i + 1] for i in range(3))
        scale = jnp.exp2(shift - shift.max(0, keepdims=True))
        total = jnp.sum(scale * (high + low), axis=0)
        numerator = jnp.sum(scale * parts_ref[:, b].astype(F32), axis=0)
        attended = numerator / total
        first.append(attended[:half])
        second.append(attended[half:])
    attended = stacked([stacked(first), stacked(second)], 1).astype(BF16)
    for i in range(out_ref.shape[0]):
        out_ref[i] = attended


def side_by_side_kernel(blocks_ref, out_ref):
    for j in range(blocks_ref.shape[0]):
        out_ref[:, j * 128 : (j + 1) * 128] = blocks_ref[j]


def project_kernel(x_ref, w_ref, out_ref):
    x = x_ref[...].reshape(-1, x_ref.shape[2])
    projected = jnp.dot(x, w_ref[...], preferred_element_type=F32)
    out_ref[...] = projected.astype(BF16).reshape(out_ref.shape)


def sum_kernel(parts_ref, out_ref):
    out_ref[...] = jnp.sum(parts_ref[...].astype(F32), axis=0).astype(BF16)


def hidden_kernel(summed_ref, stream_ref, hidden_ref, squares_ref):
    stream = stacked([stream_ref[b].astype(F32) for b in range(stream_ref.shape[0])])
    hidden = stream + summed_ref[...].astype(F32)
    hidden_ref[...] = hidden
    squares = hidden * hidden
    squares = sum(squares[:, j : j + 128] for j in range(0, squares.shape[1], 128))
    for i in range(squares_ref.shape[0]):
        squares_ref[i] = squares


def norm_kernel(squares_ref, hidden_ref, gain_ref, stream_ref, normed_ref):
    squares = jnp.sum(jnp.sum(squares_ref[...], axis=0), axis=1, keepdims=True)
    hidden = hidden_ref[...]
    normed = hidden * lax.rsqrt(squares / D + 1e-06) * gain_ref[...].astype(F32)
    rows_b, steps, _ = stream_ref.shape
    for b in range(rows_b):
        stream_ref[b] = hidden[b * steps : (b + 1) * steps].astype(BF16)
        normed_ref[b] = normed[b * steps : (b + 1) * steps].astype(BF16)


def call(kernel, outs, *args, flops=0):
    single = not isinstance(outs, list)
    size = sum(a.size * a.dtype.itemsize for a in args)
    vmem = pl.BlockSpec(memory_space=pltpu.VMEM)
    return pl.pallas_call(
        kernel,
        out_shape=outs,
        in_specs=[vmem] * len(args),
        out_specs=vmem if single else [vmem] * len(outs),
        compiler_params=pltpu.CompilerParams(vmem_limit_bytes=32 * 1024 * 1024),
        cost_estimate=pl.CostEstimate(flops=flops, bytes_accessed=size, transcendentals=0),
    )(*args)


def on_device(
    stream_in, queries, new_keys, new_values, key_cache, value_cache, lengths, out_weight, norm_gain
):
    rows_b, steps, width = queries.shape
    kv_heads, head_dim = key_cache.shape[2:]
    n_tp, n_arc = lax.axis_size("tp"), lax.axis_size(ARC)
    n_quad = lax.axis_size(QUAD)
    n_rep = n_arc * lax.axis_size("ra")
    rows = rows_b * steps
    columns = stream_in.shape[2]
    share = width // n_tp

    def place_of(arc, quad):
        return (quad - arc * n_quad + 6) % n_arc

    def columns_of(arc, place):
        return (place - 6 + arc * n_quad) % n_arc

    def weight_home(r):
        quad, member = r // n_quad, r % n_quad
        arc = (quad // n_quad - member) % n_quad
        return arc * n_arc + place_of(arc, quad)

    with jax.named_scope("weights"):
        quad = exchanged(jnp.broadcast_to(out_weight, (n_quad, *out_weight.shape)), QUAD)

    with jax.named_scope("attention"):
        flat = lambda a: a.reshape(rows_b, -1, head_dim)
        parts = attend(
            queries, flat(new_keys), flat(new_values), flat(key_cache), flat(value_cache), lengths,
            jax.ShapeDtypeStruct((n_tp, rows_b + 1, 8, head_dim), BF16),
        )
        parts, quad = lax.optimization_barrier((parts, quad))
        weight = permuted(quad, REP, n_rep, weight_home)
        weight = call(
            side_by_side_kernel, jax.ShapeDtypeStruct((share, columns), BF16), weight, flops=20_000_000_000
        )
        parts = exchanged(parts, "tp")
        attended = call(combine_kernel, jax.ShapeDtypeStruct((n_arc, rows, share), BF16), parts, flops=4_000_000_000)
        attended = exchanged(attended, ARC)

    with jax.named_scope("projection"):
        projected = call(
            project_kernel, jax.ShapeDtypeStruct((n_arc, rows, columns), BF16), attended, weight,
            flops=2 * n_arc * rows * share * columns,
        )
        partials = exchanged(projected, "tp")
        summed = call(sum_kernel, jax.ShapeDtypeStruct((rows, columns), BF16), partials)

        def home(i):
            arc, place, p = i // (n_arc * n_tp), i // n_tp % n_arc, i % n_tp
            return (arc * n_arc + p) * n_tp + columns_of(arc, place)

        summed = permuted(summed, (*REP, "tp"), n_rep * n_tp, home)

    with jax.named_scope("norm"):
        hidden, squares = call(
            hidden_kernel,
            [
                jax.ShapeDtypeStruct((rows, columns), F32),
                jax.ShapeDtypeStruct((n_tp, rows, 128), F32),
            ],
            summed, stream_in,
        )
        squares = exchanged(squares, "tp")
        out = jax.ShapeDtypeStruct(stream_in.shape, BF16)
        return tuple(call(norm_kernel, [out, out], squares, hidden, norm_gain.reshape(1, -1)))


def solution(mesh):
    finer = Mesh(mesh.devices.reshape(4, 4, 4, mesh.shape["tp"]), (*REP, "tp"))
    in_specs = (
        P(REP, None, "tp"),
        P(REP, None, None),
        P(REP, None, None, None),
        P(REP, None, None, None),
        P(REP, "tp", None, None),
        P(REP, "tp", None, None),
        P(REP),
        P("tp", REP),
        P("tp"),
    )
    out_specs = (P(REP, None, "tp"), P(REP, None, "tp"))
    return jax.shard_map(
        on_device, mesh=finer, in_specs=in_specs, out_specs=out_specs, check_vma=False
    )
```

```python
import math

import jax
import jax.numpy as jnp
from jax import lax
from jax.experimental import pallas as pl
from jax.experimental.pallas import tpu as pltpu
from jax.sharding import Mesh
from jax.sharding import PartitionSpec as P

D = 8192
REP = ("ra", "rb", "rc")
ARC = ("rb", "rc")
QUAD = "rc"
MASKED = -1e30
NONE_VISIBLE = -1e29
F32, BF16 = jnp.float32, jnp.bfloat16


def place_of(arc, quad, places=16, quads=4):
    return (quad + (places - quads) * arc + 6) % places


def columns_of(arc, place, places=16, quads=4):
    return (place + quads * arc + places - 6) % places


def exchanged(pieces, axes):
    return lax.all_to_all(pieces, axes, split_axis=0, concat_axis=0, tiled=True)


def permuted(array, axes, count, target):
    return lax.ppermute(array, axes, [(i, target(i)) for i in range(count)])


def dot_rows(a, b):
    return lax.dot_general(a, b, (((1,), (1,)), ((), ())), preferred_element_type=F32)


def stacked(pieces, axis=0):
    return jnp.concatenate(pieces, axis=axis)


def attend_kernel(len_ref, q_ref, nk_ref, nv_ref, k_ref, v_ref, out_ref, stats_ref):
    b = pl.program_id(0)
    rows_b = pl.num_programs(0)
    _, steps, width = q_ref.shape
    head_dim = k_ref.shape[2]
    kv_heads = nk_ref.shape[1] // steps
    heads = width // head_dim
    rows = heads * steps
    columns = k_ref.shape[1]
    block_len = columns // kv_heads
    to_log2 = math.log2(math.e) / math.sqrt(head_dim)
    tp = lax.axis_index("tp")

    def own_head(count):
        row = lax.broadcasted_iota(jnp.int32, (rows, count), 0)
        column = lax.broadcasted_iota(jnp.int32, (rows, count), 1)
        same = (column % kv_heads) == (row // (rows // kv_heads))
        return row, column // kv_heads, same

    def masked(key_ref, visible):
        return jnp.where(visible, dot_rows(q, key_ref[0]) * to_log2, MASKED)

    _, position, same = own_head(columns)
    visible = same & (position < len_ref[b] - tp * block_len)
    row, fresh_at, same = own_head(nk_ref.shape[1])
    fresh_visible = same & (fresh_at <= row % steps) & (tp == 0)
    wide = q_ref[0].astype(F32)
    q = stacked([wide[:, h * head_dim : (h + 1) * head_dim] for h in range(heads)]).astype(BF16)
    scores, fresh = masked(k_ref, visible), masked(nk_ref, fresh_visible)
    top = jnp.maximum(scores.max(1, keepdims=True), fresh.max(1, keepdims=True))
    shift = jnp.maximum(top, NONE_VISIBLE).astype(BF16).astype(F32)
    weights, fresh_weights = jnp.exp2(scores - shift), jnp.exp2(fresh - shift)
    total = weights.sum(1, keepdims=True) + fresh_weights.sum(1, keepdims=True)
    numerator = jnp.dot(weights.astype(BF16), v_ref[0], preferred_element_type=F32)
    numerator += jnp.dot(fresh_weights.astype(BF16), nv_ref[0], preferred_element_type=F32)
    out_ref[:, b] = numerator.astype(BF16).reshape(-1, 8, head_dim)
    high = total.astype(BF16).astype(F32)
    lane = lax.broadcasted_iota(jnp.int32, (rows, head_dim), 1)
    stats = jnp.where(b == 0, jnp.zeros((rows, head_dim), F32), stats_ref[...])
    stats = jnp.where(lane == 3 * b, shift, stats)
    stats = jnp.where(lane == 3 * b + 1, high, stats)
    stats = jnp.where(lane == 3 * b + 2, total - high, stats)
    stats_ref[...] = stats
    out_ref[:, rows_b] = stats.astype(BF16).reshape(-1, 8, head_dim)


def attend(queries, new_keys, new_values, keys, values, lengths, outs):
    def of_row(a):
        return pl.BlockSpec((1, *a.shape[1:]), lambda b: (b, 0, 0))

    return pl.pallas_call(
        attend_kernel,
        grid=(queries.shape[0],),
        out_shape=outs,
        in_specs=[
            pl.BlockSpec(memory_space=pltpu.SMEM),
            *(of_row(a) for a in (queries, new_keys, new_values, keys, values)),
        ],
        out_specs=pl.BlockSpec(outs.shape, lambda b: (0, 0, 0, 0)),
        scratch_shapes=[pltpu.VMEM((outs.shape[0] * outs.shape[2], outs.shape[3]), F32)],
        compiler_params=pltpu.CompilerParams(vmem_limit_bytes=60 * 1024 * 1024),
        cost_estimate=pl.CostEstimate(
            flops=300_000_000, bytes_accessed=2 * keys.size * 2, transcendentals=600_000
        ),
    )(lengths, queries, new_keys, new_values, keys, values)


def combine_kernel(parts_ref, out_ref):
    rows_b = parts_ref.shape[1] - 1
    half = parts_ref.shape[2] // 2
    stats = parts_ref[:, rows_b].astype(F32)
    first, second = [], []
    for b in range(rows_b):
        shift, high, low = (stats[:, :, 3 * b + i : 3 * b + i + 1] for i in range(3))
        scale = jnp.exp2(shift - shift.max(0, keepdims=True))
        total = jnp.sum(scale * (high + low), axis=0)
        numerator = jnp.sum(scale * parts_ref[:, b].astype(F32), axis=0)
        attended = numerator / total
        first.append(attended[:half])
        second.append(attended[half:])
    attended = stacked([stacked(first), stacked(second)], 1).astype(BF16)
    for i in range(out_ref.shape[0]):
        out_ref[i] = attended


def side_by_side_kernel(blocks_ref, out_ref):
    for j in range(blocks_ref.shape[0]):
        out_ref[:, j * 128 : (j + 1) * 128] = blocks_ref[j]


def project_kernel(x_ref, w_ref, out_ref):
    x = x_ref[...].reshape(-1, x_ref.shape[2])
    projected = jnp.dot(x, w_ref[...], preferred_element_type=F32)
    projected = projected.astype(BF16).reshape(out_ref.shape)
    for place in range(out_ref.shape[0]):
        out_ref[columns_of(lax.axis_index("ra"), place)] = projected[place]


def sum_kernel(parts_ref, out_ref):
    out_ref[...] = jnp.sum(parts_ref[...].astype(F32), axis=0).astype(BF16)


def hidden_kernel(summed_ref, stream_ref, hidden_ref, squares_ref):
    stream = stacked([stream_ref[b].astype(F32) for b in range(stream_ref.shape[0])])
    hidden = stream + summed_ref[...].astype(F32)
    hidden_ref[...] = hidden
    squares = hidden * hidden
    squares = sum(squares[:, j : j + 128] for j in range(0, squares.shape[1], 128))
    for i in range(squares_ref.shape[0]):
        squares_ref[i] = squares


def norm_kernel(squares_ref, hidden_ref, gain_ref, stream_ref, normed_ref):
    squares = jnp.sum(jnp.sum(squares_ref[...], axis=0), axis=1, keepdims=True)
    hidden = hidden_ref[...]
    normed = hidden * lax.rsqrt(squares / D + 1e-06) * gain_ref[...].astype(F32)
    rows_b, steps, _ = stream_ref.shape
    for b in range(rows_b):
        stream_ref[b] = hidden[b * steps : (b + 1) * steps].astype(BF16)
        normed_ref[b] = normed[b * steps : (b + 1) * steps].astype(BF16)


def call(kernel, outs, *args, flops=0):
    single = not isinstance(outs, list)
    size = sum(a.size * a.dtype.itemsize for a in args)
    vmem = pl.BlockSpec(memory_space=pltpu.VMEM)
    return pl.pallas_call(
        kernel,
        out_shape=outs,
        in_specs=[vmem] * len(args),
        out_specs=vmem if single else [vmem] * len(outs),
        compiler_params=pltpu.CompilerParams(vmem_limit_bytes=32 * 1024 * 1024),
        cost_estimate=pl.CostEstimate(flops=flops, bytes_accessed=size, transcendentals=0),
    )(*args)


def on_device(
    stream_in, queries, new_keys, new_values, key_cache, value_cache, lengths, out_weight, norm_gain
):
    rows_b, steps, width = queries.shape
    kv_heads, head_dim = key_cache.shape[2:]
    n_tp, n_arc = lax.axis_size("tp"), lax.axis_size(ARC)
    n_quad = lax.axis_size(QUAD)
    n_rep = n_arc * lax.axis_size("ra")
    rows = rows_b * steps
    columns = stream_in.shape[2]
    share = width // n_tp

    def weight_home(r):
        quad, member = r // n_quad, r % n_quad
        arc = (quad // n_quad - member) % n_quad
        return arc * n_arc + place_of(arc, quad)

    with jax.named_scope("weights"):
        quad = exchanged(jnp.broadcast_to(out_weight, (n_quad, *out_weight.shape)), QUAD)

    with jax.named_scope("attention"):
        flat = lambda a: a.reshape(rows_b, -1, head_dim)
        parts = attend(
            queries, flat(new_keys), flat(new_values), flat(key_cache), flat(value_cache), lengths,
            jax.ShapeDtypeStruct((n_tp, rows_b + 1, 8, head_dim), BF16),
        )
        parts, quad = lax.optimization_barrier((parts, quad))
        weight = permuted(quad, REP, n_rep, weight_home)
        weight = call(
            side_by_side_kernel, jax.ShapeDtypeStruct((share, columns), BF16), weight, flops=20_000_000_000
        )
        parts = exchanged(parts, "tp")
        attended = call(combine_kernel, jax.ShapeDtypeStruct((n_arc, rows, share), BF16), parts)
        attended = exchanged(attended, ARC)

    with jax.named_scope("projection"):
        projected = call(
            project_kernel, jax.ShapeDtypeStruct((n_arc, rows, columns), BF16), attended, weight,
            flops=2 * n_arc * rows * share * columns,
        )
        partials = exchanged(projected, "tp")
        summed = call(sum_kernel, jax.ShapeDtypeStruct((rows, columns), BF16), partials)

        def home(i):
            arc, place, p = i // (n_arc * n_tp), i // n_tp % n_arc, i % n_tp
            return (arc * n_arc + place_of(arc, p)) * n_tp + columns_of(arc, place)

        summed = permuted(summed, (*REP, "tp"), n_rep * n_tp, home)

    with jax.named_scope("norm"):
        hidden, squares = call(
            hidden_kernel,
            [
                jax.ShapeDtypeStruct((rows, columns), F32),
                jax.ShapeDtypeStruct((n_tp, rows, 128), F32),
            ],
            summed, stream_in,
        )
        squares = exchanged(squares, "tp")
        out = jax.ShapeDtypeStruct(stream_in.shape, BF16)
        return tuple(call(norm_kernel, [out, out], squares, hidden, norm_gain.reshape(1, -1)))


def solution(mesh):
    finer = Mesh(mesh.devices.reshape(4, 4, 4, mesh.shape["tp"]), (*REP, "tp"))
    in_specs = (
        P(REP, None, "tp"),
        P(REP, None, None),
        P(REP, None, None, None),
        P(REP, None, None, None),
        P(REP, "tp", None, None),
        P(REP, "tp", None, None),
        P(REP),
        P("tp", REP),
        P("tp"),
    )
    out_specs = (P(REP, None, "tp"), P(REP, None, "tp"))
    return jax.shard_map(
        on_device, mesh=finer, in_specs=in_specs, out_specs=out_specs, check_vma=False
    )
```

```python
import math

import jax
import jax.numpy as jnp
from jax import lax
from jax.experimental import pallas as pl
from jax.experimental.pallas import tpu as pltpu
from jax.sharding import Mesh
from jax.sharding import PartitionSpec as P

D = 8192
REP = ("ra", "rb", "rc")
ARC = ("rb", "rc")
QUAD = "rc"
MASKED = -1e30
NONE_VISIBLE = -1e29
F32, BF16 = jnp.float32, jnp.bfloat16


def exchanged(pieces, axes):
    return lax.all_to_all(pieces, axes, split_axis=0, concat_axis=0, tiled=True)


def permuted(array, axes, count, target):
    return lax.ppermute(array, axes, [(i, target(i)) for i in range(count)])


def dot_rows(a, b):
    return lax.dot_general(a, b, (((1,), (1,)), ((), ())), preferred_element_type=F32)


def stacked(pieces, axis=0):
    return jnp.concatenate(pieces, axis=axis)


def attend_kernel(len_ref, q_ref, nk_ref, nv_ref, k_ref, v_ref, out_ref, stats_ref):
    b = pl.program_id(0)
    rows_b = pl.num_programs(0)
    _, steps, width = q_ref.shape
    head_dim = k_ref.shape[2]
    kv_heads = nk_ref.shape[1] // steps
    heads = width // head_dim
    rows = heads * steps
    columns = k_ref.shape[1]
    block_len = columns // kv_heads
    to_log2 = math.log2(math.e) / math.sqrt(head_dim)
    tp = lax.axis_index("tp")

    def own_head(count):
        row = lax.broadcasted_iota(jnp.int32, (rows, count), 0)
        column = lax.broadcasted_iota(jnp.int32, (rows, count), 1)
        same = (column % kv_heads) == (row // (rows // kv_heads))
        return row, column // kv_heads, same

    def masked(key_ref, visible):
        return jnp.where(visible, dot_rows(q, key_ref[0]) * to_log2, MASKED)

    _, position, same = own_head(columns)
    visible = same & (position < len_ref[b] - tp * block_len)
    row, fresh_at, same = own_head(nk_ref.shape[1])
    fresh_visible = same & (fresh_at <= row % steps) & (tp == 0)
    wide = q_ref[0].astype(F32)
    q = stacked([wide[:, h * head_dim : (h + 1) * head_dim] for h in range(heads)]).astype(BF16)
    scores, fresh = masked(k_ref, visible), masked(nk_ref, fresh_visible)
    top = jnp.maximum(scores.max(1, keepdims=True), fresh.max(1, keepdims=True))
    shift = jnp.maximum(top, NONE_VISIBLE).astype(BF16).astype(F32)
    weights, fresh_weights = jnp.exp2(scores - shift), jnp.exp2(fresh - shift)
    total = weights.sum(1, keepdims=True) + fresh_weights.sum(1, keepdims=True)
    numerator = jnp.dot(weights.astype(BF16), v_ref[0], preferred_element_type=F32)
    numerator += jnp.dot(fresh_weights.astype(BF16), nv_ref[0], preferred_element_type=F32)
    out_ref[:, b] = numerator.astype(BF16).reshape(-1, 8, head_dim)
    high = total.astype(BF16).astype(F32)
    lane = lax.broadcasted_iota(jnp.int32, (rows, head_dim), 1)
    stats = jnp.where(b == 0, jnp.zeros((rows, head_dim), F32), stats_ref[...])
    stats = jnp.where(lane == 3 * b, shift, stats)
    stats = jnp.where(lane == 3 * b + 1, high, stats)
    stats = jnp.where(lane == 3 * b + 2, total - high, stats)
    stats_ref[...] = stats
    out_ref[:, rows_b] = stats.astype(BF16).reshape(-1, 8, head_dim)


def attend(queries, new_keys, new_values, keys, values, lengths, outs):
    def of_row(a):
        return pl.BlockSpec((1, *a.shape[1:]), lambda b: (b, 0, 0))

    return pl.pallas_call(
        attend_kernel,
        grid=(queries.shape[0],),
        out_shape=outs,
        in_specs=[
            pl.BlockSpec(memory_space=pltpu.SMEM),
            *(of_row(a) for a in (queries, new_keys, new_values, keys, values)),
        ],
        out_specs=pl.BlockSpec(outs.shape, lambda b: (0, 0, 0, 0)),
        scratch_shapes=[pltpu.VMEM((outs.shape[0] * outs.shape[2], outs.shape[3]), F32)],
        compiler_params=pltpu.CompilerParams(vmem_limit_bytes=60 * 1024 * 1024),
        cost_estimate=pl.CostEstimate(
            flops=300_000_000, bytes_accessed=2 * keys.size * 2, transcendentals=600_000
        ),
    )(lengths, queries, new_keys, new_values, keys, values)


def combine_kernel(parts_ref, out_ref):
    rows_b = parts_ref.shape[1] - 1
    half = parts_ref.shape[2] // 2
    stats = parts_ref[:, rows_b].astype(F32)
    first, second = [], []
    for b in range(rows_b):
        shift, high, low = (stats[:, :, 3 * b + i : 3 * b + i + 1] for i in range(3))
        scale = jnp.exp2(shift - shift.max(0, keepdims=True))
        total = jnp.sum(scale * (high + low), axis=0)
        numerator = jnp.sum(scale * parts_ref[:, b].astype(F32), axis=0)
        attended = numerator / total
        first.append(attended[:half])
        second.append(attended[half:])
    attended = stacked([stacked(first), stacked(second)], 1).astype(BF16)
    for i in range(out_ref.shape[0]):
        out_ref[i] = attended


def side_by_side_kernel(blocks_ref, out_ref):
    for j in range(blocks_ref.shape[0]):
        out_ref[:, j * 128 : (j + 1) * 128] = blocks_ref[j]


def project_kernel(x_ref, w_ref, out_ref):
    x = x_ref[...].reshape(-1, x_ref.shape[2])
    projected = jnp.dot(x, w_ref[...], preferred_element_type=F32)
    out_ref[...] = projected.astype(BF16).reshape(out_ref.shape)


def sum_kernel(parts_ref, out_ref):
    out_ref[...] = jnp.sum(parts_ref[...].astype(F32), axis=0).astype(BF16)


def hidden_kernel(summed_ref, stream_ref, hidden_ref, squares_ref):
    stream = stacked([stream_ref[b].astype(F32) for b in range(stream_ref.shape[0])])
    hidden = stream + summed_ref[...].astype(F32)
    hidden_ref[...] = hidden
    squares = hidden * hidden
    squares = sum(squares[:, j : j + 128] for j in range(0, squares.shape[1], 128))
    for i in range(squares_ref.shape[0]):
        squares_ref[i] = squares


def norm_kernel(squares_ref, hidden_ref, gain_ref, stream_ref, normed_ref):
    squares = jnp.sum(jnp.sum(squares_ref[...], axis=0), axis=1, keepdims=True)
    hidden = hidden_ref[...]
    normed = hidden * lax.rsqrt(squares / D + 1e-06) * gain_ref[...].astype(F32)
    rows_b, steps, _ = stream_ref.shape
    for b in range(rows_b):
        stream_ref[b] = hidden[b * steps : (b + 1) * steps].astype(BF16)
        normed_ref[b] = normed[b * steps : (b + 1) * steps].astype(BF16)


def call(kernel, outs, *args, flops=0):
    single = not isinstance(outs, list)
    size = sum(a.size * a.dtype.itemsize for a in args)
    vmem = pl.BlockSpec(memory_space=pltpu.VMEM)
    return pl.pallas_call(
        kernel,
        out_shape=outs,
        in_specs=[vmem] * len(args),
        out_specs=vmem if single else [vmem] * len(outs),
        compiler_params=pltpu.CompilerParams(vmem_limit_bytes=32 * 1024 * 1024),
        cost_estimate=pl.CostEstimate(flops=flops, bytes_accessed=size, transcendentals=0),
    )(*args)


def on_device(
    stream_in, queries, new_keys, new_values, key_cache, value_cache, lengths, out_weight, norm_gain
):
    rows_b, steps, width = queries.shape
    kv_heads, head_dim = key_cache.shape[2:]
    n_tp, n_arc = lax.axis_size("tp"), lax.axis_size(ARC)
    n_quad = lax.axis_size(QUAD)
    n_rep = n_arc * lax.axis_size("ra")
    rows = rows_b * steps
    columns = stream_in.shape[2]
    share = width // n_tp

    def swap(arc, quad):
        return (quad // n_quad - arc) % n_quad % 2

    def place_of(arc, quad):
        return (quad - arc * n_quad + 6) % n_arc ^ swap(arc, quad)

    def columns_of(arc, place):
        quad = (place - 6 + arc * n_quad) % n_arc
        return quad ^ swap(arc, quad)

    def weight_home(r):
        quad, member = r // n_quad, r % n_quad
        arc = (quad // n_quad - (member ^ quad % 2)) % n_quad
        return arc * n_arc + place_of(arc, quad)

    with jax.named_scope("weights"):
        quad = exchanged(jnp.broadcast_to(out_weight, (n_quad, *out_weight.shape)), QUAD)

    with jax.named_scope("attention"):
        flat = lambda a: a.reshape(rows_b, -1, head_dim)
        parts = attend(
            queries, flat(new_keys), flat(new_values), flat(key_cache), flat(value_cache), lengths,
            jax.ShapeDtypeStruct((n_tp, rows_b + 1, 8, head_dim), BF16),
        )
        parts, quad = lax.optimization_barrier((parts, quad))
        weight = permuted(quad, REP, n_rep, weight_home)
        weight = call(
            side_by_side_kernel, jax.ShapeDtypeStruct((share, columns), BF16), weight, flops=20_000_000_000
        )
        parts = exchanged(parts, "tp")
        attended = call(combine_kernel, jax.ShapeDtypeStruct((n_arc, rows, share), BF16), parts)
        attended = exchanged(attended, ARC)

    with jax.named_scope("projection"):
        projected = call(
            project_kernel, jax.ShapeDtypeStruct((n_arc, rows, columns), BF16), attended, weight,
            flops=2 * n_arc * rows * share * columns,
        )
        partials = exchanged(projected, "tp")
        summed = call(sum_kernel, jax.ShapeDtypeStruct((rows, columns), BF16), partials)

        def home(i):
            arc, place, p = i // (n_arc * n_tp), i // n_tp % n_arc, i % n_tp
            return (arc * n_arc + p) * n_tp + columns_of(arc, place)

        summed = permuted(summed, (*REP, "tp"), n_rep * n_tp, home)

    with jax.named_scope("norm"):
        hidden, squares = call(
            hidden_kernel,
            [
                jax.ShapeDtypeStruct((rows, columns), F32),
                jax.ShapeDtypeStruct((n_tp, rows, 128), F32),
            ],
            summed, stream_in,
        )
        squares = exchanged(squares, "tp")
        out = jax.ShapeDtypeStruct(stream_in.shape, BF16)
        return tuple(call(norm_kernel, [out, out], squares, hidden, norm_gain.reshape(1, -1)))


def solution(mesh):
    finer = Mesh(mesh.devices.reshape(4, 4, 4, mesh.shape["tp"]), (*REP, "tp"))
    in_specs = (
        P(REP, None, "tp"),
        P(REP, None, None),
        P(REP, None, None, None),
        P(REP, None, None, None),
        P(REP, "tp", None, None),
        P(REP, "tp", None, None),
        P(REP),
        P("tp", REP),
        P("tp"),
    )
    out_specs = (P(REP, None, "tp"), P(REP, None, "tp"))
    return jax.shard_map(
        on_device, mesh=finer, in_specs=in_specs, out_specs=out_specs, check_vma=False
    )
```

```python
import math

import jax
import jax.numpy as jnp
from jax import lax
from jax.experimental import pallas as pl
from jax.experimental.pallas import tpu as pltpu
from jax.sharding import Mesh
from jax.sharding import PartitionSpec as P

D = 8192
REP = ("ra", "rb", "rc")
ARC = ("rb", "rc")
QUAD = "rc"
MASKED = -1e30
NONE_VISIBLE = -1e29
F32, BF16 = jnp.float32, jnp.bfloat16


def exchanged(pieces, axes):
    return lax.all_to_all(pieces, axes, split_axis=0, concat_axis=0, tiled=True)


def permuted(array, axes, count, target):
    return lax.ppermute(array, axes, [(i, target(i)) for i in range(count)])


def dot_rows(a, b):
    return lax.dot_general(a, b, (((1,), (1,)), ((), ())), preferred_element_type=F32)


def stacked(pieces, axis=0):
    return jnp.concatenate(pieces, axis=axis)


def attend_kernel(len_ref, q_ref, nk_ref, nv_ref, k_ref, v_ref, out_ref, stats_ref):
    b = pl.program_id(0)
    rows_b = pl.num_programs(0)
    _, steps, width = q_ref.shape
    head_dim = k_ref.shape[2]
    kv_heads = nk_ref.shape[1] // steps
    heads = width // head_dim
    rows = heads * steps
    columns = k_ref.shape[1]
    block_len = columns // kv_heads
    to_log2 = math.log2(math.e) / math.sqrt(head_dim)
    tp = lax.axis_index("tp")

    def own_head(count):
        row = lax.broadcasted_iota(jnp.int32, (rows, count), 0)
        column = lax.broadcasted_iota(jnp.int32, (rows, count), 1)
        same = (column % kv_heads) == (row // (rows // kv_heads))
        return row, column // kv_heads, same

    def masked(key_ref, visible):
        return jnp.where(visible, dot_rows(q, key_ref[0]) * to_log2, MASKED)

    _, position, same = own_head(columns)
    visible = same & (position < len_ref[b] - tp * block_len)
    row, fresh_at, same = own_head(nk_ref.shape[1])
    fresh_visible = same & (fresh_at <= row % steps) & (tp == 0)
    wide = q_ref[0].astype(F32)
    q = stacked([wide[:, h * head_dim : (h + 1) * head_dim] for h in range(heads)]).astype(BF16)
    scores, fresh = masked(k_ref, visible), masked(nk_ref, fresh_visible)
    top = jnp.maximum(scores.max(1, keepdims=True), fresh.max(1, keepdims=True))
    shift = jnp.maximum(top, NONE_VISIBLE).astype(BF16).astype(F32)
    weights, fresh_weights = jnp.exp2(scores - shift), jnp.exp2(fresh - shift)
    total = weights.sum(1, keepdims=True) + fresh_weights.sum(1, keepdims=True)
    numerator = jnp.dot(weights.astype(BF16), v_ref[0], preferred_element_type=F32)
    numerator += jnp.dot(fresh_weights.astype(BF16), nv_ref[0], preferred_element_type=F32)
    out_ref[:, b] = numerator.astype(BF16).reshape(-1, 8, head_dim)
    high = total.astype(BF16).astype(F32)
    lane = lax.broadcasted_iota(jnp.int32, (rows, head_dim), 1)
    stats = jnp.where(b == 0, jnp.zeros((rows, head_dim), F32), stats_ref[...])
    stats = jnp.where(lane == 3 * b, shift, stats)
    stats = jnp.where(lane == 3 * b + 1, high, stats)
    stats = jnp.where(lane == 3 * b + 2, total - high, stats)
    stats_ref[...] = stats
    out_ref[:, rows_b] = stats.astype(BF16).reshape(-1, 8, head_dim)


def attend(queries, new_keys, new_values, keys, values, lengths, outs):
    def of_row(a):
        return pl.BlockSpec((1, *a.shape[1:]), lambda b: (b, 0, 0))

    return pl.pallas_call(
        attend_kernel,
        grid=(queries.shape[0],),
        out_shape=outs,
        in_specs=[
            pl.BlockSpec(memory_space=pltpu.SMEM),
            *(of_row(a) for a in (queries, new_keys, new_values, keys, values)),
        ],
        out_specs=pl.BlockSpec(outs.shape, lambda b: (0, 0, 0, 0)),
        scratch_shapes=[pltpu.VMEM((outs.shape[0] * outs.shape[2], outs.shape[3]), F32)],
        compiler_params=pltpu.CompilerParams(vmem_limit_bytes=60 * 1024 * 1024),
        cost_estimate=pl.CostEstimate(
            flops=300_000_000, bytes_accessed=2 * keys.size * 2, transcendentals=600_000
        ),
    )(lengths, queries, new_keys, new_values, keys, values)


def combine_kernel(parts_ref, out_ref):
    rows_b = parts_ref.shape[1] - 1
    half = parts_ref.shape[2] // 2
    stats = parts_ref[:, rows_b].astype(F32)
    first, second = [], []
    for b in range(rows_b):
        shift, high, low = (stats[:, :, 3 * b + i : 3 * b + i + 1] for i in range(3))
        scale = jnp.exp2(shift - shift.max(0, keepdims=True))
        total = jnp.sum(scale * (high + low), axis=0)
        numerator = jnp.sum(scale * parts_ref[:, b].astype(F32), axis=0)
        attended = numerator / total
        first.append(attended[:half])
        second.append(attended[half:])
    attended = stacked([stacked(first), stacked(second)], 1).astype(BF16)
    for i in range(out_ref.shape[0]):
        out_ref[i] = attended


def side_by_side_kernel(blocks_ref, out_ref):
    for j in range(blocks_ref.shape[0]):
        out_ref[:, j * 128 : (j + 1) * 128] = blocks_ref[j]


def project_kernel(x_ref, w_ref, out_ref):
    x = x_ref[...].reshape(-1, x_ref.shape[2])
    projected = jnp.dot(x, w_ref[...], preferred_element_type=F32)
    out_ref[...] = projected.astype(BF16).reshape(out_ref.shape)


def sum_kernel(parts_ref, out_ref):
    out_ref[...] = jnp.sum(parts_ref[...].astype(F32), axis=0).astype(BF16)


def hidden_kernel(summed_ref, stream_ref, hidden_ref, squares_ref):
    stream = stacked([stream_ref[b].astype(F32) for b in range(stream_ref.shape[0])])
    hidden = stream + summed_ref[...].astype(F32)
    hidden_ref[...] = hidden
    squares = hidden * hidden
    squares = sum(squares[:, j : j + 128] for j in range(0, squares.shape[1], 128))
    squares = squares[:, :64] + squares[:, 64:]
    squares = stacked([squares[:8], squares[8:]], 1)
    for i in range(squares_ref.shape[0]):
        squares_ref[i] = squares


def norm_kernel(squares_ref, hidden_ref, gain_ref, stream_ref, normed_ref):
    squares = jnp.sum(squares_ref[...], axis=0)
    squares = stacked([squares[:, :64], squares[:, 64:]])
    squares = jnp.sum(squares, axis=1, keepdims=True)
    hidden = hidden_ref[...]
    normed = hidden * lax.rsqrt(squares / D + 1e-06) * gain_ref[...].astype(F32)
    rows_b, steps, _ = stream_ref.shape
    for b in range(rows_b):
        stream_ref[b] = hidden[b * steps : (b + 1) * steps].astype(BF16)
        normed_ref[b] = normed[b * steps : (b + 1) * steps].astype(BF16)


def call(kernel, outs, *args, flops=0):
    single = not isinstance(outs, list)
    size = sum(a.size * a.dtype.itemsize for a in args)
    vmem = pl.BlockSpec(memory_space=pltpu.VMEM)
    return pl.pallas_call(
        kernel,
        out_shape=outs,
        in_specs=[vmem] * len(args),
        out_specs=vmem if single else [vmem] * len(outs),
        compiler_params=pltpu.CompilerParams(vmem_limit_bytes=32 * 1024 * 1024),
        cost_estimate=pl.CostEstimate(flops=flops, bytes_accessed=size, transcendentals=0),
    )(*args)


def on_device(
    stream_in, queries, new_keys, new_values, key_cache, value_cache, lengths, out_weight, norm_gain
):
    rows_b, steps, width = queries.shape
    kv_heads, head_dim = key_cache.shape[2:]
    n_tp, n_arc = lax.axis_size("tp"), lax.axis_size(ARC)
    n_quad = lax.axis_size(QUAD)
    n_rep = n_arc * lax.axis_size("ra")
    rows = rows_b * steps
    columns = stream_in.shape[2]
    share = width // n_tp

    def swap(arc, quad):
        return (quad // n_quad - arc) % n_quad % 2

    def place_of(arc, quad):
        return (quad - arc * n_quad + 6) % n_arc ^ swap(arc, quad)

    def columns_of(arc, place):
        quad = (place - 6 + arc * n_quad) % n_arc
        return quad ^ swap(arc, quad)

    def weight_home(r):
        quad, member = r // n_quad, r % n_quad
        arc = (quad // n_quad - (member ^ quad % 2)) % n_quad
        return arc * n_arc + place_of(arc, quad)

    with jax.named_scope("weights"):
        quad = exchanged(jnp.broadcast_to(out_weight, (n_quad, *out_weight.shape)), QUAD)

    with jax.named_scope("attention"):
        flat = lambda a: a.reshape(rows_b, -1, head_dim)
        parts = attend(
            queries, flat(new_keys), flat(new_values), flat(key_cache), flat(value_cache), lengths,
            jax.ShapeDtypeStruct((n_tp, rows_b + 1, 8, head_dim), BF16),
        )
        parts, quad = lax.optimization_barrier((parts, quad))
        weight = permuted(quad, REP, n_rep, weight_home)
        weight = call(
            side_by_side_kernel, jax.ShapeDtypeStruct((share, columns), BF16), weight, flops=20_000_000_000
        )
        parts = exchanged(parts, "tp")
        attended = call(combine_kernel, jax.ShapeDtypeStruct((n_arc, rows, share), BF16), parts)
        attended = exchanged(attended, ARC)

    with jax.named_scope("projection"):
        projected = call(
            project_kernel, jax.ShapeDtypeStruct((n_arc, rows, columns), BF16), attended, weight,
            flops=2 * n_arc * rows * share * columns,
        )
        partials = exchanged(projected, "tp")
        summed = call(sum_kernel, jax.ShapeDtypeStruct((rows, columns), BF16), partials)

        def home(i):
            arc, place, p = i // (n_arc * n_tp), i // n_tp % n_arc, i % n_tp
            return (arc * n_arc + p) * n_tp + columns_of(arc, place)

        summed = permuted(summed, (*REP, "tp"), n_rep * n_tp, home)

    with jax.named_scope("norm"):
        hidden, squares = call(
            hidden_kernel,
            [
                jax.ShapeDtypeStruct((rows, columns), F32),
                jax.ShapeDtypeStruct((n_tp, rows // 2, 128), F32),
            ],
            summed, stream_in,
        )
        squares = exchanged(squares, "tp")
        out = jax.ShapeDtypeStruct(stream_in.shape, BF16)
        return tuple(call(norm_kernel, [out, out], squares, hidden, norm_gain.reshape(1, -1)))


def solution(mesh):
    finer = Mesh(mesh.devices.reshape(4, 4, 4, mesh.shape["tp"]), (*REP, "tp"))
    in_specs = (
        P(REP, None, "tp"),
        P(REP, None, None),
        P(REP, None, None, None),
        P(REP, None, None, None),
        P(REP, "tp", None, None),
        P(REP, "tp", None, None),
        P(REP),
        P("tp", REP),
        P("tp"),
    )
    out_specs = (P(REP, None, "tp"), P(REP, None, "tp"))
    return jax.shard_map(
        on_device, mesh=finer, in_specs=in_specs, out_specs=out_specs, check_vma=False
    )
```
